768 devices in a mesh: space: 24 (over x, z_lo, core), shot: 32 (over z_hi, y).
Axes of the slice: x: 4, y: 8, z: 12 (z_hi: 4, z_lo: 3; z = z_hi * 3 + z_lo), core: 2. Of those that a mesh axis runs over, the one named last changes fastest.
Arguments:
- adjoint: float32 [32, 96, 9, 512], P('shot', 'space'), may hold values from -6 to 6
- checkpoint: bfloat16 [32, 96, 9, 512], P('shot', 'space'), may hold values from -6 to 6
- ckpt_scale: int32 [32, 96, 9], P('shot', 'space'), may hold values from -2 to 2
- lame_first: float32 [96, 512], P('space'), may hold values from 1 to 3
- shear_modulus: float32 [96, 512], P('space'), may hold values from 0.5 to 1.5
- buoyancy: float32 [96, 512], P('space'), may hold values from 0.5 to 2
- stiffness: float32 [3, 8, 8], replicated, may hold values from -2 to 2
- lts_level: int32 [96], P('space'), may hold values from 1 to 4, as said below
- neighbour_patch: int32 [96, 6], P('space'), may hold values from 0 to 95, as said below
- neighbour_face: int32 [96, 6], P('space'), may hold values from 0 to 5, as said below
- face_count: int32 [96], P('space'), may hold values from 1 to 6
Outputs:
- adjoint_prev: float32 [32, 96, 9, 512], P('shot', 'space')
- material_grad: float32 [96, 3, 512], P('space')
The draws below stay inside these ranges and needn't reach their ends.
Inputs may be any that keep to these rules, and one draw needn't show every extreme that they name: `lts_level`: each patch's substeps are 1 or 4; many more patches take 4 among the lowest-numbered quarter of patches. `neighbour_patch`: every entry differs from its own patch number by 1 to 2, and by exactly 2 in some rows. `neighbour_face`: each row is an ordering of the six faces, so the live entries of a patch name distinct faces.
All inputs are finite; a program needn't handle non-finite values.
Results may differ from the reference program's by a relative error of at most 0.0003.
Values sent between devices are 32-bit elements; how exact they have to be, the bound alone decides.
A program may use at most 32 MiB of HBM per device.

```python
import math
import jax
import jax.numpy as jnp
from jax import lax

SPLINE_EDGE = 8
NB = 512
REACH = 2
PATCHES = 96
SHOTS = 32


def draw_lts_level(key, part):
    key = jax.random.fold_in(key, 3)
    patch_ids = jnp.arange(PATCHES, dtype=jnp.int32)
    ticket = jax.random.randint(key, (PATCHES,), 0, 10, dtype=jnp.int32)
    bar = jnp.where(patch_ids < PATCHES // 4, 8, 1)
    level = jnp.where(ticket < bar, 4, 1)
    level = jnp.where(patch_ids % 5 == 0, 4, level)
    level = jnp.where(patch_ids % 5 == 1, 1, level)
    return level.astype(jnp.int32)


def draw_neighbour_patch(key, part):
    key = jax.random.fold_in(key, 5)
    key_mag, key_sign = jax.random.split(key)
    magnitude = jax.random.randint(key_mag, (PATCHES, 6), 1, REACH + 1, dtype=jnp.int32)
    sign_val = jax.random.randint(key_sign, (PATCHES, 6), 0, 2, dtype=jnp.int32) * 2 - 1
    patch_ids = jnp.arange(PATCHES, dtype=jnp.int32)[:, None]
    slot_ids = jnp.arange(6, dtype=jnp.int32)[None, :]
    magnitude = jnp.where((patch_ids % 3 == 0) & (slot_ids == 0), REACH, magnitude)
    target = patch_ids + sign_val * magnitude
    outside = (target < 0) | (target >= PATCHES)
    target = jnp.where(outside, patch_ids - sign_val * magnitude, target)
    return target.astype(jnp.int32)


def draw_neighbour_face(key, part):
    key = jax.random.fold_in(key, 7)
    row_keys = jax.random.split(key, PATCHES)
    faces = jax.vmap(lambda row_key: jax.random.permutation(row_key, jnp.arange(6, dtype=jnp.int32)))(row_keys)
    return faces.astype(jnp.int32)


def draw_face_count(key, part):
    key = jax.random.fold_in(key, 9)
    patch_ids = jnp.arange(PATCHES, dtype=jnp.int32)
    counts = jax.random.randint(key, (PATCHES,), 1, 7, dtype=jnp.int32)
    counts = jnp.where(patch_ids % 7 == 0, 6, counts)
    counts = jnp.where(patch_ids % 7 == 3, 1, counts)
    return counts.astype(jnp.int32)


def place_ends(array, rng, low, largest):
    index_at = [jax.random.randint(jax.random.fold_in(rng, axis), (), 0, length) for axis, length in enumerate(array.shape)]
    main_axis = array.shape.index(max(array.shape))
    next_to = index_at[:main_axis] + [(index_at[main_axis] + 1) % array.shape[main_axis]] + index_at[main_axis + 1:]
    return array.at[tuple(index_at)].set(low).at[tuple(next_to)].set(largest)


def block_levels(stream_key, extent, shards, smallest, top_value):
    level = 1.0
    for position, blocks in shards:
        steps = jax.random.uniform(jax.random.fold_in(jax.random.fold_in(stream_key, 6), position), (blocks,), jnp.float32, smallest / len(shards), top_value / len(shards))
        level = level * jnp.repeat(jnp.exp(steps), extent[position] // blocks).reshape((-1,) + (1,) * (len(extent) - 1 - position))
    return level


def normal_values(own_key, shape, width, limit, cuts=(), kind=jnp.bfloat16):
    loudness = block_levels(own_key, shape, cuts, -0.22, 0.18) if cuts else 1.0
    entries = jax.random.normal(own_key, shape, jnp.float32) * width * loudness
    return jnp.minimum(jnp.maximum(entries, -limit), limit).astype(kind)


def setup_inputs(seed: int = 0) -> dict:
    splits = jax.random.split(jax.random.key(seed), 12)
    adjoint = normal_values(splits[0], (SHOTS, PATCHES, 9, NB), 1.0, 6.0, ((0, 32), (1, 24)), jnp.float32)
    checkpoint = normal_values(splits[1], (SHOTS, PATCHES, 9, NB), 1.0, 6.0, ((0, 32), (1, 24)))
    ckpt_scale = place_ends(jax.random.randint(splits[2], (SHOTS, PATCHES, 9), -2, 3), jax.random.fold_in(splits[2], 1), -2, 2).astype(jnp.int32)
    lame_first = jnp.clip(jnp.exp(math.log(3.0) - 1.0986123 * jax.random.uniform(splits[3], (PATCHES, NB), jnp.float32) ** block_levels(splits[3], (PATCHES, NB), ((0, 24),), -0.2, 0.2)), 1.0, 3.0)
    shear_modulus = jnp.clip(jnp.exp(math.log(1.5) - 1.0986123 * jax.random.uniform(splits[4], (PATCHES, NB), jnp.float32) ** block_levels(splits[4], (PATCHES, NB), ((0, 24),), -0.2, 0.2)), 0.5, 1.5)
    buoyancy = jnp.clip(jnp.exp(math.log(2.0) - 1.3862944 * jax.random.uniform(splits[5], (PATCHES, NB), jnp.float32) ** block_levels(splits[5], (PATCHES, NB), ((0, 24),), -0.2, 0.2)), 0.5, 2.0)
    stiffness = normal_values(splits[6], (3, SPLINE_EDGE, SPLINE_EDGE), SPLINE_EDGE ** -0.5, 2.0, (), jnp.float32)
    lts_level = draw_lts_level(jax.random.fold_in(splits[11], 71), 0)
    neighbour_patch = draw_neighbour_patch(jax.random.fold_in(splits[11], 71), 0)
    neighbour_face = draw_neighbour_face(jax.random.fold_in(splits[11], 71), 0)
    face_count = draw_face_count(jax.random.fold_in(splits[11], 71), 0)
    return {"adjoint": adjoint, "checkpoint": checkpoint, "ckpt_scale": ckpt_scale, "lame_first": lame_first, "shear_modulus": shear_modulus, "buoyancy": buoyancy, "stiffness": stiffness, "lts_level": lts_level, "neighbour_patch": neighbour_patch, "neighbour_face": neighbour_face, "face_count": face_count}


penalty = 0.5
coarse_step = 0.2
finest_level = lax.Precision.HIGHEST

forward_forms = ("pvabc,ad->pvdbc", "pvabc,bd->pvadc", "pvabc,cd->pvabd")
transposed_forms = ("pvabc,da->pvdbc", "pvabc,db->pvadc", "pvabc,dc->pvabd")


def along_dim(stacked, matrix, form):
    patch_grid, count = stacked.shape[0], stacked.shape[1]
    cube = stacked.reshape(patch_grid, count, SPLINE_EDGE, SPLINE_EDGE, SPLINE_EDGE)
    result = jnp.einsum(form, cube, matrix, precision=finest_level)
    return result.reshape(patch_grid, count, SPLINE_EDGE * SPLINE_EDGE * SPLINE_EDGE)


def face_traces(fields):
    patch_grid = fields.shape[0]
    cube = fields.reshape(patch_grid, 9, SPLINE_EDGE, SPLINE_EDGE, SPLINE_EDGE)
    face_list = [cube[:, :, 0], cube[:, :, SPLINE_EDGE - 1], cube[:, :, :, 0], cube[:, :, :, SPLINE_EDGE - 1], cube[:, :, :, :, 0], cube[:, :, :, :, SPLINE_EDGE - 1]]
    return jnp.stack([face.reshape(patch_grid, 9 * SPLINE_EDGE * SPLINE_EDGE) for face in face_list], axis=1)


def face_lift(local_faces, partner, neighbour_face, face_count):
    patch_grid = local_faces.shape[0]
    slot_ids = jnp.arange(6, dtype=jnp.int32)
    indicator_vector = (neighbour_face[:, :, None] == slot_ids[None, None, :]).astype(jnp.float32)
    live_mask = (slot_ids[None, :] < face_count[:, None]).astype(jnp.float32)
    local_match = jnp.einsum("auh,ahd->aud", indicator_vector, local_faces, precision=finest_level)
    jump_flux = penalty * live_mask[:, :, None] * (partner - local_match)
    face_indicator = jnp.einsum("anl,ans->als", indicator_vector, jump_flux, precision=finest_level).reshape(patch_grid, 6, 9, SPLINE_EDGE, SPLINE_EDGE)
    cube = jnp.zeros((patch_grid, 9, SPLINE_EDGE, SPLINE_EDGE, SPLINE_EDGE), jnp.float32)
    cube = cube.at[:, :, 0].add(face_indicator[:, 0])
    cube = cube.at[:, :, SPLINE_EDGE - 1].add(face_indicator[:, 1])
    cube = cube.at[:, :, :, 0].add(face_indicator[:, 2])
    cube = cube.at[:, :, :, SPLINE_EDGE - 1].add(face_indicator[:, 3])
    cube = cube.at[:, :, :, :, 0].add(face_indicator[:, 4])
    cube = cube.at[:, :, :, :, SPLINE_EDGE - 1].add(face_indicator[:, 5])
    return cube.reshape(patch_grid, 9, SPLINE_EDGE * SPLINE_EDGE * SPLINE_EDGE)


pair_index = ((0, 5, 4), (5, 1, 3), (4, 3, 2))


def forward_slopes(forward, stiffness):
    slopes = []
    for j in range(3):
        stacked = jnp.stack([forward[:, 0], forward[:, 1], forward[:, 2], forward[:, 3 + pair_index[0][j]], forward[:, 3 + pair_index[1][j]], forward[:, 3 + pair_index[2][j]]], axis=1)
        slopes.append(along_dim(stacked, stiffness[j], forward_forms[j]))
    return slopes


def adjoint_rate(adj_state, lame_first, shear_modulus, buoyancy, stiffness):
    stress = adj_state[:, 3:9]
    stress_trace = stress[:, 0] + stress[:, 1] + stress[:, 2]
    scaled_vel = buoyancy[:, None] * adj_state[:, 0:3]
    results = []
    for j in range(3):
        stress_terms = []
        for i in range(3):
            term = 2.0 * shear_modulus * stress[:, pair_index[i][j]]
            if i == j:
                term = term + lame_first * stress_trace
            stress_terms.append(term)
        stacked = jnp.stack(stress_terms + [scaled_vel[:, 0], scaled_vel[:, 1], scaled_vel[:, 2]], axis=1)
        results.append(along_dim(stacked, stiffness[j], transposed_forms[j]))
    rate_vel = [results[0][:, i] + results[1][:, i] + results[2][:, i] for i in range(3)]
    rate_stress = [results[0][:, 3], results[1][:, 4], results[2][:, 5],
                   results[2][:, 4] + results[1][:, 5],
                   results[2][:, 3] + results[0][:, 5],
                   results[1][:, 3] + results[0][:, 4]]
    return jnp.stack(rate_vel + rate_stress, axis=1)


def gradient_rate(adj_state, slopes):
    stress = adj_state[:, 3:9]
    stress_trace = stress[:, 0] + stress[:, 1] + stress[:, 2]
    divergence = slopes[0][:, 0] + slopes[1][:, 1] + slopes[2][:, 2]
    grad_lame = stress_trace * divergence
    grad_shear = 2.0 * (stress[:, 0] * slopes[0][:, 0] + stress[:, 1] * slopes[1][:, 1] + stress[:, 2] * slopes[2][:, 2])
    grad_shear = grad_shear + stress[:, 3] * (slopes[2][:, 1] + slopes[1][:, 2])
    grad_shear = grad_shear + stress[:, 4] * (slopes[2][:, 0] + slopes[0][:, 2])
    grad_shear = grad_shear + stress[:, 5] * (slopes[1][:, 0] + slopes[0][:, 1])
    grad_buoy = adj_state[:, 0] * (slopes[0][:, 3] + slopes[1][:, 3] + slopes[2][:, 3])
    grad_buoy = grad_buoy + adj_state[:, 1] * (slopes[0][:, 4] + slopes[1][:, 4] + slopes[2][:, 4])
    grad_buoy = grad_buoy + adj_state[:, 2] * (slopes[0][:, 5] + slopes[1][:, 5] + slopes[2][:, 5])
    return jnp.stack([grad_lame, grad_shear, grad_buoy], axis=1)


def reverse_window(adj_state, lifted, forward, lame_first, shear_modulus, buoyancy, stiffness, lts_level, combine_sum):
    slopes = forward_slopes(forward, stiffness)
    level_float = lts_level.astype(jnp.float32)
    summed = jnp.zeros((adj_state.shape[0], 3, adj_state.shape[2]), jnp.float32)
    for substep in range(4):
        sub_step = jnp.where(substep < lts_level, coarse_step / level_float, jnp.float32(0.0))[:, None, None]
        contrib = sub_step * gradient_rate(adj_state, slopes)
        summed = summed + combine_sum(contrib)
        adj_state = adj_state + sub_step * (adjoint_rate(adj_state, lame_first, shear_modulus, buoyancy, stiffness) + lifted)
    return adj_state, summed


def decode(stored, exponent):
    return stored.astype(jnp.float32) * jnp.exp2(exponent.astype(jnp.float32))[:, :, None]


def reference(adjoint, checkpoint, ckpt_scale, lame_first, shear_modulus, buoyancy, stiffness, lts_level, neighbour_patch, neighbour_face, face_count):
    row_index = (neighbour_patch * 6 + jnp.bitwise_xor(neighbour_face, 1)).astype(jnp.int32)

    def one_shot(summed, shot_data):
        adj_state, stored, exponent = shot_data
        forward = decode(stored, exponent)
        local_faces = face_traces(adj_state)
        partner = local_faces.reshape(-1, 9 * SPLINE_EDGE * SPLINE_EDGE)[row_index]
        lifted = face_lift(local_faces, partner, neighbour_face, face_count)
        new_state, grads = reverse_window(adj_state, lifted, forward, lame_first, shear_modulus, buoyancy, stiffness, lts_level, lambda value: value)
        return summed + grads, new_state

    start_sum = jnp.zeros((adjoint.shape[1], 3, adjoint.shape[3]), jnp.float32)
    summed, states = lax.scan(one_shot, start_sum, (adjoint, checkpoint, ckpt_scale))
    return states, summed
```

```python
import functools

import jax
import jax.numpy as jnp
from jax import lax
from jax.experimental import pallas as pl
from jax.experimental.pallas import tpu as pltpu
from jax.sharding import PartitionSpec as P

ROWS = 8
LANES = 128
FIELDS = 9
GROUP = 8
PAIR = ((0, 5, 4), (5, 1, 3), (4, 3, 2))
MESH = pl.DeviceIdType.MESH
F32 = jnp.float32
BF16 = jnp.bfloat16


def row_roll(x, shift):
    return pltpu.roll(x, shift % ROWS, 0)


def lane_roll(x, shift):
    return pltpu.roll(x, shift % LANES, 1)


def split_dot(pieces, weights):
    x = jnp.concatenate(pieces, axis=0)
    high = x.astype(BF16)
    low = (x - high.astype(F32)).astype(BF16)
    out = jnp.dot(jnp.concatenate([high, low], axis=1), weights, preferred_element_type=F32)
    out = out[:, :LANES] + out[:, LANES:]
    return [out[ROWS * i : ROWS * (i + 1)] for i in range(len(pieces))]


def along_first(pair, table):
    out = [None, None]
    for t in range(2):
        turned = lane_roll(pair[t], 64)
        for r, base in enumerate((pair[t], turned)):
            swapped = row_roll(base, 4)
            for s, value in enumerate((base, swapped)):
                for u in range(2):
                    term = table[((u * 2 + t) * 2 + r) * 2 + s] * value
                    out[u] = term if out[u] is None else out[u] + term
    return out


def derivatives(groups, table, weights_mid, weights_last):
    first = [along_first(pair, table) for pair in groups[0]]
    results = [first]
    for j, weights in ((1, weights_mid), (2, weights_last)):
        flat = split_dot([tile for pair in groups[j] for tile in pair], weights)
        results.append([[flat[2 * i], flat[2 * i + 1]] for i in range(len(groups[j]))])
    return results


def rate_of(state, lam, mu2, buo, table, weights_mid, weights_last):
    tiles = range(2)
    stress = state[3:]
    scaled = [[mu2[t] * stress[k][t] for t in tiles] for k in range(6)]
    for t in tiles:
        bulk = lam[t] * (stress[0][t] + stress[1][t] + stress[2][t])
        for k in range(3):
            scaled[k][t] = scaled[k][t] + bulk
    moved = [[buo[t] * state[i][t] for t in tiles] for i in range(3)]
    groups = [[scaled[PAIR[i][j]] for i in range(3)] + moved for j in range(3)]
    r = derivatives(groups, table, weights_mid, weights_last)
    out = [[r[0][i][t] + r[1][i][t] + r[2][i][t] for t in tiles] for i in range(3)]
    out += [r[0][3], r[1][4], r[2][5]]
    out.append([r[2][4][t] + r[1][5][t] for t in tiles])
    out.append([r[2][3][t] + r[0][5][t] for t in tiles])
    out.append([r[1][3][t] + r[0][4][t] for t in tiles])
    return out


def kernel(
    n_space,
    n_shot,
    adj_hbm,
    ckpt_hbm,
    scale_hbm,
    lam_hbm,
    mu_hbm,
    buo_hbm,
    stiff_hbm,
    level_hbm,
    npatch_hbm,
    nface_hbm,
    count_hbm,
    out_adj,
    out_grad,
    adj_v,
    ckpt_v,
    ckpt_f,
    lam_v,
    mu_v,
    buo_v,
    scale_s,
    stiff_s,
    level_s,
    npatch_s,
    nface_s,
    count_s,
    state_v,
    sum_v,
    slope_v,
    fwd_v,
    mix_v,
    lift_v,
    coef_v,
    own_v,
    step_v,
    mat_v,
    table_v,
    weight_v,
    send_left,
    send_right,
    from_left,
    from_right,
    grad_v,
    part_v,
    level_part_v,
    total_v,
    result_v,
    in_sem,
    halo_send,
    halo_recv,
    scatter_send,
    scatter_recv,
    cross_send,
    cross_recv,
    gather_send,
    gather_recv,
    out_sem,
):
    n_far = n_shot // GROUP
    space = lax.axis_index("space")
    shot = lax.axis_index("shot")
    far, near = shot // GROUP, lax.rem(shot, GROUP)
    right, left = lax.rem(space + 1, n_space), lax.rem(space + n_space - 1, n_space)
    near_peers = [lax.rem(near + k, GROUP) for k in range(GROUP)]
    far_peers = [lax.rem(far + k, n_far) for k in range(n_far)]

    def at_shot(far_index, near_index):
        return (space, far_index * GROUP + near_index)

    barrier = pltpu.get_barrier_semaphore()
    for device in (
        [(left, shot), (right, shot)]
        + [at_shot(far, near_peers[k]) for k in range(1, GROUP)]
        + [at_shot(far_peers[k], near) for k in range(1, n_far)]
    ):
        pl.semaphore_signal(barrier, inc=1, device_id=device, device_id_type=MESH)

    loads = [
        pltpu.make_async_copy(source, target, in_sem.at[i])
        for i, (source, target) in enumerate(
            (
                (adj_hbm.at[0], adj_v),
                (ckpt_hbm.at[0], ckpt_v),
                (lam_hbm, lam_v),
                (mu_hbm, mu_v),
                (buo_hbm, buo_v),
                (scale_hbm, scale_s),
                (stiff_hbm, stiff_s),
                (level_hbm, level_s),
                (npatch_hbm, npatch_s),
                (nface_hbm, nface_s),
                (count_hbm, count_s),
            )
        )
    ]
    for load in loads:
        load.start()

    row = lax.broadcasted_iota(jnp.int32, (ROWS, LANES), 0)
    lane = lax.broadcasted_iota(jnp.int32, (ROWS, LANES), 1)
    patch = row & 3
    half = row >> 2
    side = lane >> 6
    mid = (lane >> 3) & 7
    last = lane & 7

    def by_patch(values):
        out = jnp.where(patch == 0, values[0], values[1])
        out = jnp.where(patch == 2, values[2], out)
        return jnp.where(patch == 3, values[3], out)

    def by_row(ref, field, t):
        out = None
        for h in range(2):
            for p in range(4):
                start = (2 * h + t) * LANES
                line = jnp.broadcast_to(ref[p, field : field + 1, start : start + LANES], (ROWS, LANES))
                out = line if out is None else jnp.where(row == 4 * h + p, line, out)
        return out

    loads[0].wait()
    for f in range(FIELDS):
        for t in range(2):
            state_v[f, t] = by_row(adj_v, f, t)
    for i in range(5):
        for t in range(2):
            even = state_v[2 * i, t]
            odd = state_v[2 * i + 1, t] if 2 * i + 1 < FIELDS else even
            send_right[i, t] = jnp.where(patch < 2, row_roll(even, -2), odd)
            send_left[i, t] = jnp.where(patch < 2, odd, row_roll(even, 2))

    for load in loads[1:]:
        load.wait()

    first_patch = 4 * space
    here = first_patch + patch
    entries = [
        (
            by_patch([nface_s[p, k] for p in range(4)]),
            by_patch([npatch_s[p, k] for p in range(4)]) - here,
        )
        for k in range(6)
    ]
    live_count = by_patch([count_s[p] for p in range(4)])
    offsets = []
    for f in range(6):
        offset = jnp.zeros((ROWS, LANES), jnp.int32)
        for k in range(6):
            face, distance = entries[k]
            offset = jnp.where((face == f) & (k < live_count), distance, offset)
        offsets.append(offset)
    even_patch = (patch & 1) == 0
    low_patch = patch < 2
    candidates = (
        jnp.where(even_patch, 1, -1),
        jnp.where(low_patch, 2, -2),
        jnp.where(even_patch, -1, 1),
        jnp.where(low_patch, -2, 2),
    )
    zero = jnp.zeros((ROWS, LANES), F32)
    first_low = [(half == 0) & (side == 0), None]
    first_high = [None, (half == 1) & (side == 1)]
    for n, wanted in enumerate(candidates):
        weight = [jnp.where(offsets[f] == wanted, 0.5, 0.0) for f in range(6)]
        coef_v[n, 0] = jnp.where(first_low[0], weight[1], zero)
        coef_v[n, 1] = jnp.where(first_high[1], weight[0], zero)
        coef_v[n, 2] = jnp.where(mid == 7, weight[2], jnp.where(mid == 0, weight[3], zero))
        coef_v[n, 3] = jnp.where(last == 7, weight[4], jnp.where(last == 0, weight[5], zero))
    live = [jnp.where(offsets[f] != 0, 0.5, 0.0) for f in range(6)]
    own_rest = (
        jnp.where(mid == 0, live[2], zero)
        + jnp.where(mid == 7, live[3], zero)
        + jnp.where(last == 0, live[4], zero)
        + jnp.where(last == 7, live[5], zero)
    )
    own_v[0] = own_rest + jnp.where(first_low[0], live[0], zero)
    own_v[1] = own_rest + jnp.where(first_high[1], live[1], zero)

    level = by_patch([level_s[p] for p in range(4)])
    step = 0.2 / level.astype(F32)
    for m in range(4):
        step_v[m] = jnp.where(m < level, step, zero)
    for n, (ref, factor) in enumerate(((lam_v, 1.0), (mu_v, 2.0), (buo_v, 1.0))):
        for t in range(2):
            low = ref[:, t * LANES : (t + 1) * LANES]
            high = ref[:, (2 + t) * LANES : (3 + t) * LANES]
            mat_v[n, t] = jnp.concatenate([low, high], axis=0) * factor
    for kind in range(2):
        for u in range(2):
            for t in range(2):
                for r in range(2):
                    for s in range(2):
                        picks = []
                        for h in range(2):
                            for e in range(2):
                                source = 4 * (h ^ s) + 2 * t + (e ^ r)
                                target = 4 * h + 2 * u + e
                                if kind == 0:
                                    picks.append(stiff_s[0, target, source])
                                else:
                                    picks.append(stiff_s[0, source, target])
                        low = jnp.where(side == 0, picks[0], picks[1])
                        high = jnp.where(side == 0, picks[2], picks[3])
                        table_v[kind, ((u * 2 + t) * 2 + r) * 2 + s] = jnp.where(half == 0, low, high)

    tall = lax.broadcasted_iota(jnp.int32, (LANES, LANES), 0)
    wide = lax.broadcasted_iota(jnp.int32, (LANES, LANES), 1)
    mid_mask = ((tall >> 6) == (wide >> 6)) & ((tall & 7) == (wide & 7))
    last_mask = (tall >> 3) == (wide >> 3)
    for kind in range(2):
        for n in range(2):
            j = n + 1
            place = mid if n == 0 else last
            spread = zero
            for a in range(8):
                line = zero
                for d in range(8):
                    value = stiff_s[j, d, a] if kind == 0 else stiff_s[j, a, d]
                    line = jnp.where(place == d, value, line)
                spread = jnp.where(row == a, line, spread)
            if n == 0:
                square = jnp.concatenate(
                    [jnp.broadcast_to(spread[a : a + 1], (ROWS, LANES)) for a in range(8)] * 2, axis=0
                )
                square = jnp.where(mid_mask, square, 0.0)
            else:
                square = jnp.where(last_mask, jnp.concatenate([spread] * 16, axis=0), 0.0)
            high = square.astype(BF16)
            low = (square - high.astype(F32)).astype(BF16)
            weight_v[kind, n, :LANES, :LANES] = high
            weight_v[kind, n, LANES:, :LANES] = high
            weight_v[kind, n, :LANES, LANES:] = low
            weight_v[kind, n, LANES:, LANES:] = low

    pl.semaphore_wait(barrier, 2 + (GROUP - 1) + (n_far - 1))
    halo = [
        pltpu.make_async_remote_copy(
            src_ref=source,
            dst_ref=target,
            send_sem=halo_send.at[i],
            recv_sem=halo_recv.at[i],
            device_id=(device, shot),
            device_id_type=MESH,
        )
        for i, (source, target, device) in enumerate(
            ((send_right, from_left, right), (send_left, from_right, left))
        )
    ]
    for copy in halo:
        copy.start()

    def get(ref):
        return [[ref[f, t] for t in range(2)] for f in range(FIELDS)]

    def adjoint_rate(state):
        return rate_of(
            state,
            [mat_v[0, t] for t in range(2)],
            [mat_v[1, t] for t in range(2)],
            [mat_v[2, t] for t in range(2)],
            [table_v[0, i] for i in range(16)],
            weight_v[0, 0],
            weight_v[0, 1],
        )

    for f in range(FIELDS):
        for t in range(2):
            x = state_v[f, t]
            back, ahead = row_roll(x, -1), row_roll(x, 1)
            inner = (
                jnp.where(even_patch, back, ahead),
                jnp.where(low_patch, row_roll(x, -2), row_roll(x, 2)),
                jnp.where((patch == 0) | (patch == 3), zero, jnp.where(patch == 1, back, ahead)),
            )
            for axis in range(3):
                slot = t if axis == 0 else axis + 1
                mix_v[axis, f, t] = sum(coef_v[n, slot] * inner[n] for n in range(3))
    start = get(state_v)
    rate = adjoint_rate(start)
    for f in range(FIELDS):
        for t in range(2):
            x = start[f][t]
            sum_v[f, t] = step_v[0] * x
            lift_v[f, t] = -own_v[t] * x
            state_v[f, t] = x + step_v[0] * rate[f][t]

    ckpt_f[...] = ckpt_v[...].astype(F32)
    for f in range(FIELDS):
        power = by_patch([scale_s[0, p, f] for p in range(4)])
        power = lax.shift_left(jnp.ones((ROWS, LANES), jnp.int32), power + 2).astype(F32) * 0.25
        for t in range(2):
            fwd_v[f, t] = by_row(ckpt_f, f, t) * power
    fields = get(fwd_v)
    groups = [fields[:3] + [fields[3 + PAIR[i][j]] for i in range(3)] for j in range(3)]
    d = derivatives(groups, [table_v[1, i] for i in range(16)], weight_v[1, 0], weight_v[1, 1])
    for t in range(2):
        slope_v[0, t] = d[0][0][t] + d[1][1][t] + d[2][2][t]
        slope_v[1, t] = 2.0 * d[0][0][t]
        slope_v[2, t] = 2.0 * d[1][1][t]
        slope_v[3, t] = 2.0 * d[2][2][t]
        slope_v[4, t] = d[2][1][t] + d[1][2][t]
        slope_v[5, t] = d[2][0][t] + d[0][2][t]
        slope_v[6, t] = d[1][0][t] + d[0][1][t]
        for i in range(3):
            slope_v[7 + i, t] = d[0][3 + i][t] + d[1][3 + i][t] + d[2][3 + i][t]

    for copy in halo:
        copy.wait()
    outer_patch = (patch == 0) | (patch == 3)
    for f in range(FIELDS):
        mixed = []
        for t in range(2):
            from_l, from_r = from_left[f // 2, t], from_right[f // 2, t]
            if f % 2 == 0:
                two = jnp.where(low_patch, from_l, from_r)
            else:
                two = jnp.where(low_patch, from_r, from_l)
                two = jnp.where(low_patch, row_roll(two, -2), row_roll(two, 2))
            one = jnp.where(patch == 0, row_roll(two, -1), row_roll(two, 1))
            one = jnp.where(outer_patch, one, zero)
            terms = []
            for axis in range(3):
                slot = t if axis == 0 else axis + 1
                terms.append(mix_v[axis, f, t] + coef_v[3, slot] * two + coef_v[2, slot] * one)
            mixed.append(terms)
        for t in range(2):
            across = row_roll(lane_roll(mixed[1 - t][0], 64), 4)
            y, z = mixed[t][1], mixed[t][2]
            y = jnp.where(mid == 0, lane_roll(y, -56), jnp.where(mid == 7, lane_roll(y, 56), zero))
            z = jnp.where(last == 0, lane_roll(z, -7), jnp.where(last == 7, lane_roll(z, 7), zero))
            lift = lift_v[f, t] + across + y + z
            lift_v[f, t] = lift
            state_v[f, t] = state_v[f, t] + step_v[0] * lift

    def advance(m):
        state = get(state_v)
        rate = adjoint_rate(state)
        for f in range(FIELDS):
            for t in range(2):
                x = state[f][t]
                if m < 3:
                    sum_v[f, t] = sum_v[f, t] + step_v[m] * x
                state_v[f, t] = x + step_v[m] * (rate[f][t] + lift_v[f, t])

    advance(1)
    advance(2)

    for t in range(2):
        a = [sum_v[f, t] + step_v[3] * state_v[f, t] for f in range(FIELDS)]
        rows = (
            (a[3] + a[4] + a[5]) * slope_v[0, t],
            sum(a[3 + k] * slope_v[1 + k, t] for k in range(6)),
            sum(a[i] * slope_v[7 + i, t] for i in range(3)),
        )
        for g, value in enumerate(rows):
            for h in range(2):
                for p in range(4):
                    begin = (2 * h + t) * LANES
                    grad_v[p, g : g + 1, begin : begin + LANES] = value[4 * h + p : 4 * h + p + 1]

    def piece(ref, index):
        return ref.at[index // 2, :, pl.ds(pl.multiple_of(lax.rem(index, 2) * 256, 256), 256)]

    scatter = [
        pltpu.make_async_remote_copy(
            src_ref=piece(grad_v, near_peers[k]),
            dst_ref=part_v.at[k],
            send_sem=scatter_send.at[k],
            recv_sem=scatter_recv.at[k],
            device_id=at_shot(far, near_peers[k]),
            device_id_type=MESH,
        )
        for k in range(1, GROUP)
    ]
    for copy in scatter:
        copy.start()

    advance(3)
    for f in range(FIELDS):
        for t in range(2):
            for h in range(2):
                for p in range(4):
                    begin = (2 * h + t) * LANES
                    r = 4 * h + p
                    result_v[p, f : f + 1, begin : begin + LANES] = state_v[f, t, r : r + 1, :]
    store = pltpu.make_async_copy(result_v, out_adj.at[0], out_sem.at[0])
    store.start()

    for copy in scatter:
        copy.wait_recv()
    mine = grad_v[near // 2, :, pl.ds(pl.multiple_of(lax.rem(near, 2) * 256, 256), 256)]
    for k in range(1, GROUP):
        mine = mine + part_v[k]
    level_part_v[far] = mine
    cross = [
        pltpu.make_async_remote_copy(
            src_ref=level_part_v.at[far],
            dst_ref=level_part_v.at[far],
            send_sem=cross_send.at[k],
            recv_sem=cross_recv.at[k],
            device_id=at_shot(far_peers[k], near),
            device_id_type=MESH,
        )
        for k in range(1, n_far)
    ]
    for copy in cross:
        copy.start()
    for copy in cross:
        copy.wait_recv()
    total = level_part_v[0]
    for k in range(1, n_far):
        total = total + level_part_v[k]
    total_v[...] = total
    gather = [
        pltpu.make_async_remote_copy(
            src_ref=total_v,
            dst_ref=piece(out_grad, near),
            send_sem=gather_send.at[k],
            recv_sem=gather_recv.at[k],
            device_id=at_shot(far, near_peers[k]),
            device_id_type=MESH,
        )
        for k in range(1, GROUP)
    ]
    for copy in gather:
        copy.start()
    keep = pltpu.make_async_copy(total_v, piece(out_grad, near), out_sem.at[1])
    keep.start()
    for copy in scatter + cross:
        copy.wait_send()
    store.wait()
    keep.wait()
    for copy in gather:
        copy.wait()


def shards(n_space, n_shot, *operands):
    adjoint, material = operands[0], operands[3]
    n_patch, n_coef = material.shape
    n_far = n_shot // GROUP
    field = (FIELDS, 2, ROWS, LANES)
    halo = (5, 2, ROWS, LANES)
    dma = pltpu.SemaphoreType.DMA
    return pl.pallas_call(
        functools.partial(kernel, n_space, n_shot),
        out_shape=(
            jax.ShapeDtypeStruct(adjoint.shape, F32),
            jax.ShapeDtypeStruct((n_patch, 3, n_coef), F32),
        ),
        in_specs=[pl.BlockSpec(memory_space=pl.ANY)] * 11,
        out_specs=[pl.BlockSpec(memory_space=pl.ANY)] * 2,
        scratch_shapes=[
            pltpu.VMEM((n_patch, FIELDS, n_coef), F32),
            pltpu.VMEM((n_patch, FIELDS, n_coef), BF16),
            pltpu.VMEM((n_patch, FIELDS, n_coef), F32),
            pltpu.VMEM((n_patch, n_coef), F32),
            pltpu.VMEM((n_patch, n_coef), F32),
            pltpu.VMEM((n_patch, n_coef), F32),
            pltpu.SMEM((1, n_patch, FIELDS), jnp.int32),
            pltpu.SMEM((3, 8, 8), F32),
            pltpu.SMEM((n_patch,), jnp.int32),
            pltpu.SMEM((n_patch, 6), jnp.int32),
            pltpu.SMEM((n_patch, 6), jnp.int32),
            pltpu.SMEM((n_patch,), jnp.int32),
            pltpu.VMEM(field, F32),
            pltpu.VMEM(field, F32),
            pltpu.VMEM((10, 2, ROWS, LANES), F32),
            pltpu.VMEM(field, F32),
            pltpu.VMEM((3,) + field, F32),
            pltpu.VMEM(field, F32),
            pltpu.VMEM((4, 4, ROWS, LANES), F32),
            pltpu.VMEM((2, ROWS, LANES), F32),
            pltpu.VMEM((4, ROWS, LANES), F32),
            pltpu.VMEM((3, 2, ROWS, LANES), F32),
            pltpu.VMEM((2, 16, ROWS, LANES), F32),
            pltpu.VMEM((2, 2, 2 * LANES, 2 * LANES), BF16),
            pltpu.VMEM(halo, F32),
            pltpu.VMEM(halo, F32),
            pltpu.VMEM(halo, F32),
            pltpu.VMEM(halo, F32),
            pltpu.VMEM((n_patch, 3, n_coef), F32),
            pltpu.VMEM((GROUP, 3, 256), F32),
            pltpu.VMEM((n_far, 3, 256), F32),
            pltpu.VMEM((3, 256), F32),
            pltpu.VMEM((n_patch, FIELDS, n_coef), F32),
            dma((11,)),
            dma((2,)),
            dma((2,)),
            dma((GROUP,)),
            dma((GROUP,)),
            dma((n_far,)),
            dma((n_far,)),
            dma((GROUP,)),
            dma((GROUP,)),
            dma((2,)),
        ],
        compiler_params=pltpu.CompilerParams(collective_id=0, has_side_effects=True),
    )(*operands)


def solution(mesh):
    return jax.shard_map(
        functools.partial(shards, mesh.shape["space"], mesh.shape["shot"]),
        mesh=mesh,
        in_specs=(
            P("shot", "space", None, None),
            P("shot", "space", None, None),
            P("shot", "space", None),
            P("space", None),
            P("space", None),
            P("space", None),
            P(),
            P("space"),
            P("space", None),
            P("space", None),
            P("space"),
        ),
        out_specs=(P("shot", "space", None, None), P("space", None, None)),
        check_vma=False,
    )
```

```python
import functools

import jax
import jax.numpy as jnp
from jax import lax
from jax.experimental import pallas as pl
from jax.experimental.pallas import tpu as pltpu
from jax.sharding import PartitionSpec as P

ROWS = 8
LANES = 128
FIELDS = 9
GROUP = 8
PAIR = ((0, 5, 4), (5, 1, 3), (4, 3, 2))
MESH = pl.DeviceIdType.MESH
F32 = jnp.float32
BF16 = jnp.bfloat16


def row_roll(x, shift):
    return pltpu.roll(x, shift % ROWS, 0)


def lane_roll(x, shift):
    return pltpu.roll(x, shift % LANES, 1)


def split_dot(pieces, weights):
    x = jnp.concatenate(pieces, axis=0)
    high = x.astype(BF16)
    low = (x - high.astype(F32)).astype(BF16)
    out = jnp.dot(jnp.concatenate([high, low], axis=1), weights, preferred_element_type=F32)
    out = out[:, :LANES] + out[:, LANES:]
    return [out[ROWS * i : ROWS * (i + 1)] for i in range(len(pieces))]


def along_first(pair, table):
    out = [None, None]
    for t in range(2):
        turned = lane_roll(pair[t], 64)
        for r, base in enumerate((pair[t], turned)):
            swapped = row_roll(base, 4)
            for s, value in enumerate((base, swapped)):
                for u in range(2):
                    term = table[((u * 2 + t) * 2 + r) * 2 + s] * value
                    out[u] = term if out[u] is None else out[u] + term
    return out


def derivatives(groups, table, weights_mid, weights_last):
    first = [along_first(pair, table) for pair in groups[0]]
    results = [first]
    for j, weights in ((1, weights_mid), (2, weights_last)):
        flat = split_dot([tile for pair in groups[j] for tile in pair], weights)
        results.append([[flat[2 * i], flat[2 * i + 1]] for i in range(len(groups[j]))])
    return results


def rate_of(state, lam, mu2, buo, table, weights_mid, weights_last):
    tiles = range(2)
    stress = state[3:]
    scaled = [[mu2[t] * stress[k][t] for t in tiles] for k in range(6)]
    for t in tiles:
        bulk = lam[t] * (stress[0][t] + stress[1][t] + stress[2][t])
        for k in range(3):
            scaled[k][t] = scaled[k][t] + bulk
    moved = [[buo[t] * state[i][t] for t in tiles] for i in range(3)]
    groups = [[scaled[PAIR[i][j]] for i in range(3)] + moved for j in range(3)]
    r = derivatives(groups, table, weights_mid, weights_last)
    out = [[r[0][i][t] + r[1][i][t] + r[2][i][t] for t in tiles] for i in range(3)]
    out += [r[0][3], r[1][4], r[2][5]]
    out.append([r[2][4][t] + r[1][5][t] for t in tiles])
    out.append([r[2][3][t] + r[0][5][t] for t in tiles])
    out.append([r[1][3][t] + r[0][4][t] for t in tiles])
    return out


def kernel(
    n_space,
    n_shot,
    adj_hbm,
    ckpt_hbm,
    scale_hbm,
    lam_hbm,
    mu_hbm,
    buo_hbm,
    stiff_hbm,
    level_hbm,
    npatch_hbm,
    nface_hbm,
    count_hbm,
    out_adj,
    out_grad,
    adj_v,
    ckpt_v,
    ckpt_f,
    lam_v,
    mu_v,
    buo_v,
    scale_s,
    stiff_s,
    level_s,
    npatch_s,
    nface_s,
    count_s,
    state_v,
    sum_v,
    slope_v,
    fwd_v,
    mix_v,
    lift_v,
    coef_v,
    own_v,
    step_v,
    mat_v,
    table_v,
    weight_v,
    send_left,
    send_right,
    from_left,
    from_right,
    grad_v,
    near_v,
    far_v,
    result_v,
    in_sem,
    halo_send,
    halo_recv,
    near_send,
    near_recv,
    far_send,
    far_recv,
    out_sem,
):
    n_far = n_shot // GROUP
    space = lax.axis_index("space")
    shot = lax.axis_index("shot")
    far, near = shot // GROUP, lax.rem(shot, GROUP)
    right, left = lax.rem(space + 1, n_space), lax.rem(space + n_space - 1, n_space)
    near_peers = [lax.rem(near + k, GROUP) for k in range(GROUP)]
    far_peers = [lax.rem(far + k, n_far) for k in range(n_far)]

    def at_shot(far_index, near_index):
        return (space, far_index * GROUP + near_index)

    barrier = pltpu.get_barrier_semaphore()
    for device in (
        [(left, shot), (right, shot)]
        + [at_shot(far, near_peers[k]) for k in range(1, GROUP)]
        + [at_shot(far_peers[k], near) for k in range(1, n_far)]
    ):
        pl.semaphore_signal(barrier, inc=1, device_id=device, device_id_type=MESH)

    loads = [
        pltpu.make_async_copy(source, target, in_sem.at[i])
        for i, (source, target) in enumerate(
            (
                (adj_hbm.at[0], adj_v),
                (ckpt_hbm.at[0], ckpt_v),
                (lam_hbm, lam_v),
                (mu_hbm, mu_v),
                (buo_hbm, buo_v),
                (scale_hbm, scale_s),
                (stiff_hbm, stiff_s),
                (level_hbm, level_s),
                (npatch_hbm, npatch_s),
                (nface_hbm, nface_s),
                (count_hbm, count_s),
            )
        )
    ]
    for load in loads:
        load.start()

    row = lax.broadcasted_iota(jnp.int32, (ROWS, LANES), 0)
    lane = lax.broadcasted_iota(jnp.int32, (ROWS, LANES), 1)
    patch = row & 3
    half = row >> 2
    side = lane >> 6
    mid = (lane >> 3) & 7
    last = lane & 7

    def by_patch(values):
        out = jnp.where(patch == 0, values[0], values[1])
        out = jnp.where(patch == 2, values[2], out)
        return jnp.where(patch == 3, values[3], out)

    def tile(ref, t):
        low = ref[:, t * LANES : (t + 1) * LANES]
        high = ref[:, (2 + t) * LANES : (3 + t) * LANES]
        return jnp.concatenate([low, high], axis=0)

    loads[0].wait()
    for f in range(FIELDS):
        for t in range(2):
            state_v[f, t] = tile(adj_v.at[f], t)
    for i in range(5):
        for t in range(2):
            even = state_v[2 * i, t]
            odd = state_v[2 * i + 1, t] if 2 * i + 1 < FIELDS else even
            send_right[i, t] = jnp.where(patch < 2, row_roll(even, -2), odd)
            send_left[i, t] = jnp.where(patch < 2, odd, row_roll(even, 2))

    pl.semaphore_wait(barrier, 2 + (GROUP - 1) + (n_far - 1))
    halo = [
        pltpu.make_async_remote_copy(
            src_ref=source,
            dst_ref=target,
            send_sem=halo_send.at[i],
            recv_sem=halo_recv.at[i],
            device_id=(device, shot),
            device_id_type=MESH,
        )
        for i, (source, target, device) in enumerate(
            ((send_right, from_left, right), (send_left, from_right, left))
        )
    ]
    for copy in halo:
        copy.start()

    for load in loads[1:]:
        load.wait()

    first_patch = 4 * space
    here = first_patch + patch
    entries = [
        (
            by_patch([nface_s[p, k] for p in range(4)]),
            by_patch([npatch_s[p, k] for p in range(4)]) - here,
        )
        for k in range(6)
    ]
    live_count = by_patch([count_s[p] for p in range(4)])
    offsets = []
    for f in range(6):
        offset = jnp.zeros((ROWS, LANES), jnp.int32)
        for k in range(6):
            face, distance = entries[k]
            offset = jnp.where((face == f) & (k < live_count), distance, offset)
        offsets.append(offset)
    even_patch = (patch & 1) == 0
    low_patch = patch < 2
    candidates = (
        jnp.where(even_patch, 1, -1),
        jnp.where(low_patch, 2, -2),
        jnp.where(even_patch, -1, 1),
        jnp.where(low_patch, -2, 2),
    )
    zero = jnp.zeros((ROWS, LANES), F32)
    first_low = [(half == 0) & (side == 0), None]
    first_high = [None, (half == 1) & (side == 1)]
    for n, wanted in enumerate(candidates):
        weight = [jnp.where(offsets[f] == wanted, 0.5, 0.0) for f in range(6)]
        coef_v[n, 0] = jnp.where(first_low[0], weight[1], zero)
        coef_v[n, 1] = jnp.where(first_high[1], weight[0], zero)
        coef_v[n, 2] = jnp.where(mid == 7, weight[2], jnp.where(mid == 0, weight[3], zero))
        coef_v[n, 3] = jnp.where(last == 7, weight[4], jnp.where(last == 0, weight[5], zero))
    live = [jnp.where(offsets[f] != 0, 0.5, 0.0) for f in range(6)]
    own_rest = (
        jnp.where(mid == 0, live[2], zero)
        + jnp.where(mid == 7, live[3], zero)
        + jnp.where(last == 0, live[4], zero)
        + jnp.where(last == 7, live[5], zero)
    )
    own_v[0] = own_rest + jnp.where(first_low[0], live[0], zero)
    own_v[1] = own_rest + jnp.where(first_high[1], live[1], zero)

    level = by_patch([level_s[p] for p in range(4)])
    step = 0.2 / level.astype(F32)
    for m in range(4):
        step_v[m] = jnp.where(m < level, step, zero)
    for n, (ref, factor) in enumerate(((lam_v, 1.0), (mu_v, 2.0), (buo_v, 1.0))):
        for t in range(2):
            mat_v[n, t] = tile(ref, t) * factor
    for kind in range(2):
        for u in range(2):
            for t in range(2):
                for r in range(2):
                    for s in range(2):
                        picks = []
                        for h in range(2):
                            for e in range(2):
                                source = 4 * (h ^ s) + 2 * t + (e ^ r)
                                target = 4 * h + 2 * u + e
                                if kind == 0:
                                    picks.append(stiff_s[0, target, source])
                                else:
                                    picks.append(stiff_s[0, source, target])
                        low = jnp.where(side == 0, picks[0], picks[1])
                        high = jnp.where(side == 0, picks[2], picks[3])
                        table_v[kind, ((u * 2 + t) * 2 + r) * 2 + s] = jnp.where(half == 0, low, high)

    tall = lax.broadcasted_iota(jnp.int32, (LANES, LANES), 0)
    wide = lax.broadcasted_iota(jnp.int32, (LANES, LANES), 1)
    mid_mask = ((tall >> 6) == (wide >> 6)) & ((tall & 7) == (wide & 7))
    last_mask = (tall >> 3) == (wide >> 3)
    for kind in range(2):
        for n in range(2):
            j = n + 1
            place = mid if n == 0 else last
            spread = zero
            for a in range(8):
                line = zero
                for d in range(8):
                    value = stiff_s[j, d, a] if kind == 0 else stiff_s[j, a, d]
                    line = jnp.where(place == d, value, line)
                spread = jnp.where(row == a, line, spread)
            if n == 0:
                square = jnp.concatenate(
                    [jnp.broadcast_to(spread[a : a + 1], (ROWS, LANES)) for a in range(8)] * 2, axis=0
                )
                square = jnp.where(mid_mask, square, 0.0)
            else:
                square = jnp.where(last_mask, jnp.concatenate([spread] * 16, axis=0), 0.0)
            high = square.astype(BF16)
            low = (square - high.astype(F32)).astype(BF16)
            weight_v[kind, n, :LANES, :LANES] = high
            weight_v[kind, n, LANES:, :LANES] = high
            weight_v[kind, n, :LANES, LANES:] = low
            weight_v[kind, n, LANES:, LANES:] = low

    def get(ref):
        return [[ref[f, t] for t in range(2)] for f in range(FIELDS)]

    def adjoint_rate(state):
        return rate_of(
            state,
            [mat_v[0, t] for t in range(2)],
            [mat_v[1, t] for t in range(2)],
            [mat_v[2, t] for t in range(2)],
            [table_v[0, i] for i in range(16)],
            weight_v[0, 0],
            weight_v[0, 1],
        )

    for f in range(FIELDS):
        for t in range(2):
            x = state_v[f, t]
            back, ahead = row_roll(x, -1), row_roll(x, 1)
            inner = (
                jnp.where(even_patch, back, ahead),
                jnp.where(low_patch, row_roll(x, -2), row_roll(x, 2)),
                jnp.where((patch == 0) | (patch == 3), zero, jnp.where(patch == 1, back, ahead)),
            )
            for axis in range(3):
                slot = t if axis == 0 else axis + 1
                mix_v[axis, f, t] = sum(coef_v[n, slot] * inner[n] for n in range(3))
    start = get(state_v)
    rate = adjoint_rate(start)
    for f in range(FIELDS):
        for t in range(2):
            x = start[f][t]
            sum_v[f, t] = step_v[0] * x
            lift_v[f, t] = -own_v[t] * x
            state_v[f, t] = x + step_v[0] * rate[f][t]

    ckpt_f[...] = ckpt_v[...].astype(F32)
    for f in range(FIELDS):
        power = by_patch([scale_s[0, p, f] for p in range(4)])
        power = lax.shift_left(jnp.ones((ROWS, LANES), jnp.int32), power + 2).astype(F32) * 0.25
        for t in range(2):
            fwd_v[f, t] = tile(ckpt_f.at[f], t) * power
    fields = get(fwd_v)
    groups = [fields[:3] + [fields[3 + PAIR[i][j]] for i in range(3)] for j in range(3)]
    d = derivatives(groups, [table_v[1, i] for i in range(16)], weight_v[1, 0], weight_v[1, 1])
    for t in range(2):
        slope_v[0, t] = d[0][0][t] + d[1][1][t] + d[2][2][t]
        slope_v[1, t] = 2.0 * d[0][0][t]
        slope_v[2, t] = 2.0 * d[1][1][t]
        slope_v[3, t] = 2.0 * d[2][2][t]
        slope_v[4, t] = d[2][1][t] + d[1][2][t]
        slope_v[5, t] = d[2][0][t] + d[0][2][t]
        slope_v[6, t] = d[1][0][t] + d[0][1][t]
        for i in range(3):
            slope_v[7 + i, t] = d[0][3 + i][t] + d[1][3 + i][t] + d[2][3 + i][t]

    for copy in halo:
        copy.wait()
    outer_patch = (patch == 0) | (patch == 3)
    for f in range(FIELDS):
        mixed = []
        for t in range(2):
            from_l, from_r = from_left[f // 2, t], from_right[f // 2, t]
            if f % 2 == 0:
                two = jnp.where(low_patch, from_l, from_r)
            else:
                two = jnp.where(low_patch, from_r, from_l)
                two = jnp.where(low_patch, row_roll(two, -2), row_roll(two, 2))
            one = jnp.where(patch == 0, row_roll(two, -1), row_roll(two, 1))
            one = jnp.where(outer_patch, one, zero)
            terms = []
            for axis in range(3):
                slot = t if axis == 0 else axis + 1
                terms.append(mix_v[axis, f, t] + coef_v[3, slot] * two + coef_v[2, slot] * one)
            mixed.append(terms)
        for t in range(2):
            across = row_roll(lane_roll(mixed[1 - t][0], 64), 4)
            y, z = mixed[t][1], mixed[t][2]
            y = jnp.where(mid == 0, lane_roll(y, -56), jnp.where(mid == 7, lane_roll(y, 56), zero))
            z = jnp.where(last == 0, lane_roll(z, -7), jnp.where(last == 7, lane_roll(z, 7), zero))
            lift = lift_v[f, t] + across + y + z
            lift_v[f, t] = lift
            state_v[f, t] = state_v[f, t] + step_v[0] * lift

    def advance(m):
        state = get(state_v)
        rate = adjoint_rate(state)
        for f in range(FIELDS):
            for t in range(2):
                x = state[f][t]
                if m < 3:
                    sum_v[f, t] = sum_v[f, t] + step_v[m] * x
                state_v[f, t] = x + step_v[m] * (rate[f][t] + lift_v[f, t])

    advance(1)
    advance(2)

    for t in range(2):
        a = [sum_v[f, t] + step_v[3] * state_v[f, t] for f in range(FIELDS)]
        rows = (
            (a[3] + a[4] + a[5]) * slope_v[0, t],
            sum(a[3 + k] * slope_v[1 + k, t] for k in range(6)),
            sum(a[i] * slope_v[7 + i, t] for i in range(3)),
        )
        for g in range(3):
            if t == 0:
                near_v[0, near, g] = rows[g]
            else:
                far_v[0, far, g] = rows[g]

    def share_far(n):
        copies = [
            pltpu.make_async_remote_copy(
                src_ref=far_v.at[n, far],
                dst_ref=far_v.at[n, far],
                send_sem=far_send.at[n, k],
                recv_sem=far_recv.at[n, k],
                device_id=at_shot(far_peers[k], near),
                device_id_type=MESH,
            )
            for k in sorted(range(1, n_far), key=lambda k: -min(k, n_far - k))
        ]
        for copy in copies:
            copy.start()
        return copies

    def share_near(n):
        copies = [
            pltpu.make_async_remote_copy(
                src_ref=near_v.at[n, near],
                dst_ref=near_v.at[n, near],
                send_sem=near_send.at[n, k],
                recv_sem=near_recv.at[n, k],
                device_id=at_shot(far, near_peers[k]),
                device_id_type=MESH,
            )
            for k in sorted(range(1, GROUP), key=lambda k: -min(k, GROUP - k))
        ]
        for copy in copies:
            copy.start()
        return copies

    def total(ref, n, count, g):
        out = ref[n, 0, g]
        for k in range(1, count):
            out = out + ref[n, k, g]
        return out

    far_one = share_far(0)
    near_one = share_near(0)

    advance(3)
    for f in range(FIELDS):
        for t in range(2):
            for h in range(2):
                begin = (2 * h + t) * LANES
                result_v[f, :, begin : begin + LANES] = state_v[f, t, 4 * h : 4 * h + 4, :]
    store = pltpu.make_async_copy(result_v, out_adj.at[0], out_sem.at[0])
    store.start()

    for copy in near_one:
        copy.wait_recv()
    for g in range(3):
        far_v[1, far, g] = total(near_v, 0, GROUP, g)
    far_two = share_far(1)
    for copy in far_one:
        copy.wait_recv()
    for g in range(3):
        near_v[1, near, g] = total(far_v, 0, n_far, g)
    near_two = share_near(1)

    for t, copies, ref, count in ((0, far_two, far_v, n_far), (1, near_two, near_v, GROUP)):
        for copy in copies:
            copy.wait_recv()
        for g in range(3):
            value = total(ref, 1, count, g)
            for h in range(2):
                begin = (2 * h + t) * LANES
                grad_v[g, :, begin : begin + LANES] = value[4 * h : 4 * h + 4]
    keep = pltpu.make_async_copy(grad_v, out_grad, out_sem.at[1])
    keep.start()
    for copy in far_one + near_one + far_two + near_two:
        copy.wait_send()
    store.wait()
    keep.wait()


def shards(n_space, n_shot, *operands):
    material = operands[3]
    n_patch, n_coef = material.shape
    n_far = n_shot // GROUP
    field = (FIELDS, 2, ROWS, LANES)
    halo = (5, 2, ROWS, LANES)
    dma = pltpu.SemaphoreType.DMA
    adjoint, checkpoint = (x.transpose(0, 2, 1, 3) for x in operands[:2])
    new_state, grads = pl.pallas_call(
        functools.partial(kernel, n_space, n_shot),
        out_shape=(
            jax.ShapeDtypeStruct((1, FIELDS, n_patch, n_coef), F32),
            jax.ShapeDtypeStruct((3, n_patch, n_coef), F32),
        ),
        in_specs=[pl.BlockSpec(memory_space=pl.ANY)] * 11,
        out_specs=[pl.BlockSpec(memory_space=pl.ANY)] * 2,
        scratch_shapes=[
            pltpu.VMEM((FIELDS, n_patch, n_coef), F32),
            pltpu.VMEM((FIELDS, n_patch, n_coef), BF16),
            pltpu.VMEM((FIELDS, n_patch, n_coef), F32),
            pltpu.VMEM((n_patch, n_coef), F32),
            pltpu.VMEM((n_patch, n_coef), F32),
            pltpu.VMEM((n_patch, n_coef), F32),
            pltpu.SMEM((1, n_patch, FIELDS), jnp.int32),
            pltpu.SMEM((3, 8, 8), F32),
            pltpu.SMEM((n_patch,), jnp.int32),
            pltpu.SMEM((n_patch, 6), jnp.int32),
            pltpu.SMEM((n_patch, 6), jnp.int32),
            pltpu.SMEM((n_patch,), jnp.int32),
            pltpu.VMEM(field, F32),
            pltpu.VMEM(field, F32),
            pltpu.VMEM((10, 2, ROWS, LANES), F32),
            pltpu.VMEM(field, F32),
            pltpu.VMEM((3,) + field, F32),
            pltpu.VMEM(field, F32),
            pltpu.VMEM((4, 4, ROWS, LANES), F32),
            pltpu.VMEM((2, ROWS, LANES), F32),
            pltpu.VMEM((4, ROWS, LANES), F32),
            pltpu.VMEM((3, 2, ROWS, LANES), F32),
            pltpu.VMEM((2, 16, ROWS, LANES), F32),
            pltpu.VMEM((2, 2, 2 * LANES, 2 * LANES), BF16),
            pltpu.VMEM(halo, F32),
            pltpu.VMEM(halo, F32),
            pltpu.VMEM(halo, F32),
            pltpu.VMEM(halo, F32),
            pltpu.VMEM((3, n_patch, n_coef), F32),
            pltpu.VMEM((2, GROUP, 3, ROWS, LANES), F32),
            pltpu.VMEM((2, n_far, 3, ROWS, LANES), F32),
            pltpu.VMEM((FIELDS, n_patch, n_coef), F32),
            dma((11,)),
            dma((2,)),
            dma((2,)),
            dma((2, GROUP)),
            dma((2, GROUP)),
            dma((2, n_far)),
            dma((2, n_far)),
            dma((2,)),
        ],
        compiler_params=pltpu.CompilerParams(collective_id=0, has_side_effects=True),
    )(adjoint, checkpoint, *operands[2:])
    return new_state.transpose(0, 2, 1, 3), grads.transpose(1, 0, 2)


def solution(mesh):
    return jax.shard_map(
        functools.partial(shards, mesh.shape["space"], mesh.shape["shot"]),
        mesh=mesh,
        in_specs=(
            P("shot", "space", None, None),
            P("shot", "space", None, None),
            P("shot", "space", None),
            P("space", None),
            P("space", None),
            P("space", None),
            P(),
            P("space"),
            P("space", None),
            P("space", None),
            P("space"),
        ),
        out_specs=(P("shot", "space", None, None), P("space", None, None)),
        check_vma=False,
    )
```

```python
import functools

import jax
import jax.numpy as jnp
from jax import lax
from jax.experimental import pallas as pl
from jax.experimental.pallas import tpu as pltpu
from jax.sharding import PartitionSpec as P

ROWS = 8
LANES = 128
FIELDS = 9
GROUP = 8
PAIR = ((0, 5, 4), (5, 1, 3), (4, 3, 2))
MESH = pl.DeviceIdType.MESH
F32 = jnp.float32
BF16 = jnp.bfloat16


def row_roll(x, shift):
    return pltpu.roll(x, shift % ROWS, 0)


def lane_roll(x, shift):
    return pltpu.roll(x, shift % LANES, 1)


def split_dot(pieces, weights):
    x = jnp.concatenate(pieces, axis=0)
    high = x.astype(BF16)
    low = (x - high.astype(F32)).astype(BF16)
    out = jnp.dot(jnp.concatenate([high, low], axis=1), weights, preferred_element_type=F32)
    out = out[:, :LANES] + out[:, LANES:]
    return [out[ROWS * i : ROWS * (i + 1)] for i in range(len(pieces))]


def along_first(pair, table):
    out = [None, None]
    for t in range(2):
        turned = lane_roll(pair[t], 64)
        for r, base in enumerate((pair[t], turned)):
            swapped = row_roll(base, 4)
            for s, value in enumerate((base, swapped)):
                for u in range(2):
                    term = table[((u * 2 + t) * 2 + r) * 2 + s] * value
                    out[u] = term if out[u] is None else out[u] + term
    return out


def derivatives(groups, table, weights_mid, weights_last):
    first = [along_first(pair, table) for pair in groups[0]]
    results = [first]
    for j, weights in ((1, weights_mid), (2, weights_last)):
        flat = split_dot([tile for pair in groups[j] for tile in pair], weights)
        results.append([[flat[2 * i], flat[2 * i + 1]] for i in range(len(groups[j]))])
    return results


def rate_of(state, lam, mu2, buo, table, weights_mid, weights_last):
    tiles = range(2)
    stress = state[3:]
    scaled = [[mu2[t] * stress[k][t] for t in tiles] for k in range(6)]
    for t in tiles:
        bulk = lam[t] * (stress[0][t] + stress[1][t] + stress[2][t])
        for k in range(3):
            scaled[k][t] = scaled[k][t] + bulk
    moved = [[buo[t] * state[i][t] for t in tiles] for i in range(3)]
    groups = [[scaled[PAIR[i][j]] for i in range(3)] + moved for j in range(3)]
    r = derivatives(groups, table, weights_mid, weights_last)
    out = [[r[0][i][t] + r[1][i][t] + r[2][i][t] for t in tiles] for i in range(3)]
    out += [r[0][3], r[1][4], r[2][5]]
    out.append([r[2][4][t] + r[1][5][t] for t in tiles])
    out.append([r[2][3][t] + r[0][5][t] for t in tiles])
    out.append([r[1][3][t] + r[0][4][t] for t in tiles])
    return out


def kernel(
    n_space,
    n_shot,
    adj_hbm,
    ckpt_hbm,
    scale_hbm,
    lam_hbm,
    mu_hbm,
    buo_hbm,
    stiff_hbm,
    level_hbm,
    npatch_hbm,
    nface_hbm,
    count_hbm,
    out_adj,
    out_grad,
    adj_v,
    ckpt_v,
    ckpt_f,
    lam_v,
    mu_v,
    buo_v,
    scale_s,
    stiff_s,
    level_s,
    npatch_s,
    nface_s,
    count_s,
    state_v,
    sum_v,
    slope_v,
    fwd_v,
    mix_v,
    lift_v,
    coef_v,
    own_v,
    step_v,
    mat_v,
    table_v,
    weight_v,
    send_left,
    send_right,
    from_left,
    from_right,
    near_v,
    far_v,
    in_sem,
    halo_send,
    halo_recv,
    near_send,
    near_recv,
    far_send,
    far_recv,
):
    n_far = n_shot // GROUP
    space = lax.axis_index("space")
    shot = lax.axis_index("shot")
    far, near = shot // GROUP, lax.rem(shot, GROUP)
    right, left = lax.rem(space + 1, n_space), lax.rem(space + n_space - 1, n_space)
    near_peers = [lax.rem(near + k, GROUP) for k in range(GROUP)]
    far_peers = [lax.rem(far + k, n_far) for k in range(n_far)]

    def at_shot(far_index, near_index):
        return (space, far_index * GROUP + near_index)

    barrier = pltpu.get_barrier_semaphore()
    for device in (
        [(left, shot), (right, shot)]
        + [at_shot(far, near_peers[k]) for k in range(1, GROUP)]
        + [at_shot(far_peers[k], near) for k in range(1, n_far)]
    ):
        pl.semaphore_signal(barrier, inc=1, device_id=device, device_id_type=MESH)

    loads = [
        pltpu.make_async_copy(source, target, in_sem.at[i])
        for i, (source, target) in enumerate(
            (
                (adj_hbm.at[0], adj_v),
                (ckpt_hbm.at[0], ckpt_v),
                (lam_hbm, lam_v),
                (mu_hbm, mu_v),
                (buo_hbm, buo_v),
                (scale_hbm, scale_s),
                (stiff_hbm, stiff_s),
                (level_hbm, level_s),
                (npatch_hbm, npatch_s),
                (nface_hbm, nface_s),
                (count_hbm, count_s),
            )
        )
    ]
    for load in loads:
        load.start()

    row = lax.broadcasted_iota(jnp.int32, (ROWS, LANES), 0)
    lane = lax.broadcasted_iota(jnp.int32, (ROWS, LANES), 1)
    patch = row & 3
    half = row >> 2
    side = lane >> 6
    mid = (lane >> 3) & 7
    last = lane & 7

    def by_patch(values):
        out = jnp.where(patch == 0, values[0], values[1])
        out = jnp.where(patch == 2, values[2], out)
        return jnp.where(patch == 3, values[3], out)

    def tile(ref, t):
        low = ref[:, t * LANES : (t + 1) * LANES]
        high = ref[:, (2 + t) * LANES : (3 + t) * LANES]
        return jnp.concatenate([low, high], axis=0)

    loads[0].wait()
    for f in range(FIELDS):
        for t in range(2):
            state_v[f, t] = tile(adj_v.at[f], t)
    for i in range(5):
        for t in range(2):
            even = state_v[2 * i, t]
            odd = state_v[2 * i + 1, t] if 2 * i + 1 < FIELDS else even
            send_right[i, t] = jnp.where(patch < 2, row_roll(even, -2), odd)
            send_left[i, t] = jnp.where(patch < 2, odd, row_roll(even, 2))

    pl.semaphore_wait(barrier, 2 + (GROUP - 1) + (n_far - 1))
    halo = [
        pltpu.make_async_remote_copy(
            src_ref=source,
            dst_ref=target,
            send_sem=halo_send.at[i],
            recv_sem=halo_recv.at[i],
            device_id=(device, shot),
            device_id_type=MESH,
        )
        for i, (source, target, device) in enumerate(
            ((send_right, from_left, right), (send_left, from_right, left))
        )
    ]
    for copy in halo:
        copy.start()

    for load in loads[1:]:
        load.wait()

    first_patch = 4 * space
    here = first_patch + patch
    entries = [
        (
            by_patch([nface_s[p, k] for p in range(4)]),
            by_patch([npatch_s[p, k] for p in range(4)]) - here,
        )
        for k in range(6)
    ]
    live_count = by_patch([count_s[p] for p in range(4)])
    offsets = []
    for f in range(6):
        offset = jnp.zeros((ROWS, LANES), jnp.int32)
        for k in range(6):
            face, distance = entries[k]
            offset = jnp.where((face == f) & (k < live_count), distance, offset)
        offsets.append(offset)
    even_patch = (patch & 1) == 0
    low_patch = patch < 2
    candidates = (
        jnp.where(even_patch, 1, -1),
        jnp.where(low_patch, 2, -2),
        jnp.where(even_patch, -1, 1),
        jnp.where(low_patch, -2, 2),
    )
    zero = jnp.zeros((ROWS, LANES), F32)
    first_low = [(half == 0) & (side == 0), None]
    first_high = [None, (half == 1) & (side == 1)]
    for n, wanted in enumerate(candidates):
        weight = [jnp.where(offsets[f] == wanted, 0.5, 0.0) for f in range(6)]
        coef_v[n, 0] = jnp.where(first_low[0], weight[1], zero)
        coef_v[n, 1] = jnp.where(first_high[1], weight[0], zero)
        coef_v[n, 2] = jnp.where(mid == 7, weight[2], jnp.where(mid == 0, weight[3], zero))
        coef_v[n, 3] = jnp.where(last == 7, weight[4], jnp.where(last == 0, weight[5], zero))
    live = [jnp.where(offsets[f] != 0, 0.5, 0.0) for f in range(6)]
    own_rest = (
        jnp.where(mid == 0, live[2], zero)
        + jnp.where(mid == 7, live[3], zero)
        + jnp.where(last == 0, live[4], zero)
        + jnp.where(last == 7, live[5], zero)
    )
    own_v[0] = own_rest + jnp.where(first_low[0], live[0], zero)
    own_v[1] = own_rest + jnp.where(first_high[1], live[1], zero)

    level = by_patch([level_s[p] for p in range(4)])
    step = 0.2 / level.astype(F32)
    for m in range(4):
        step_v[m] = jnp.where(m < level, step, zero)
    for n, (ref, factor) in enumerate(((lam_v, 1.0), (mu_v, 2.0), (buo_v, 1.0))):
        for t in range(2):
            mat_v[n, t] = tile(ref, t) * factor
    for kind in range(2):
        for u in range(2):
            for t in range(2):
                for r in range(2):
                    for s in range(2):
                        picks = []
                        for h in range(2):
                            for e in range(2):
                                source = 4 * (h ^ s) + 2 * t + (e ^ r)
                                target = 4 * h + 2 * u + e
                                if kind == 0:
                                    picks.append(stiff_s[0, target, source])
                                else:
                                    picks.append(stiff_s[0, source, target])
                        low = jnp.where(side == 0, picks[0], picks[1])
                        high = jnp.where(side == 0, picks[2], picks[3])
                        table_v[kind, ((u * 2 + t) * 2 + r) * 2 + s] = jnp.where(half == 0, low, high)

    tall = lax.broadcasted_iota(jnp.int32, (LANES, LANES), 0)
    wide = lax.broadcasted_iota(jnp.int32, (LANES, LANES), 1)
    mid_mask = ((tall >> 6) == (wide >> 6)) & ((tall & 7) == (wide & 7))
    last_mask = (tall >> 3) == (wide >> 3)
    for kind in range(2):
        for n in range(2):
            j = n + 1
            place = mid if n == 0 else last
            spread = zero
            for a in range(8):
                line = zero
                for d in range(8):
                    value = stiff_s[j, d, a] if kind == 0 else stiff_s[j, a, d]
                    line = jnp.where(place == d, value, line)
                spread = jnp.where(row == a, line, spread)
            if n == 0:
                square = jnp.concatenate(
                    [jnp.broadcast_to(spread[a : a + 1], (ROWS, LANES)) for a in range(8)] * 2, axis=0
                )
                square = jnp.where(mid_mask, square, 0.0)
            else:
                square = jnp.where(last_mask, jnp.concatenate([spread] * 16, axis=0), 0.0)
            high = square.astype(BF16)
            low = (square - high.astype(F32)).astype(BF16)
            weight_v[kind, n, :LANES, :LANES] = high
            weight_v[kind, n, LANES:, :LANES] = high
            weight_v[kind, n, :LANES, LANES:] = low
            weight_v[kind, n, LANES:, LANES:] = low

    def get(ref):
        return [[ref[f, t] for t in range(2)] for f in range(FIELDS)]

    def adjoint_rate(state):
        return rate_of(
            state,
            [mat_v[0, t] for t in range(2)],
            [mat_v[1, t] for t in range(2)],
            [mat_v[2, t] for t in range(2)],
            [table_v[0, i] for i in range(16)],
            weight_v[0, 0],
            weight_v[0, 1],
        )

    for f in range(FIELDS):
        for t in range(2):
            x = state_v[f, t]
            back, ahead = row_roll(x, -1), row_roll(x, 1)
            inner = (
                jnp.where(even_patch, back, ahead),
                jnp.where(low_patch, row_roll(x, -2), row_roll(x, 2)),
                jnp.where((patch == 0) | (patch == 3), zero, jnp.where(patch == 1, back, ahead)),
            )
            for axis in range(3):
                slot = t if axis == 0 else axis + 1
                mix_v[axis, f, t] = sum(coef_v[n, slot] * inner[n] for n in range(3))
    start = get(state_v)
    rate = adjoint_rate(start)
    for f in range(FIELDS):
        for t in range(2):
            x = start[f][t]
            sum_v[f, t] = step_v[0] * x
            lift_v[f, t] = -own_v[t] * x
            state_v[f, t] = x + step_v[0] * rate[f][t]

    ckpt_f[...] = ckpt_v[...].astype(F32)
    for f in range(FIELDS):
        power = by_patch([scale_s[0, p, f] for p in range(4)])
        power = lax.shift_left(jnp.ones((ROWS, LANES), jnp.int32), power + 2).astype(F32) * 0.25
        for t in range(2):
            fwd_v[f, t] = tile(ckpt_f.at[f], t) * power
    fields = get(fwd_v)
    groups = [fields[:3] + [fields[3 + PAIR[i][j]] for i in range(3)] for j in range(3)]
    d = derivatives(groups, [table_v[1, i] for i in range(16)], weight_v[1, 0], weight_v[1, 1])
    for t in range(2):
        slope_v[0, t] = d[0][0][t] + d[1][1][t] + d[2][2][t]
        slope_v[1, t] = 2.0 * d[0][0][t]
        slope_v[2, t] = 2.0 * d[1][1][t]
        slope_v[3, t] = 2.0 * d[2][2][t]
        slope_v[4, t] = d[2][1][t] + d[1][2][t]
        slope_v[5, t] = d[2][0][t] + d[0][2][t]
        slope_v[6, t] = d[1][0][t] + d[0][1][t]
        for i in range(3):
            slope_v[7 + i, t] = d[0][3 + i][t] + d[1][3 + i][t] + d[2][3 + i][t]

    for copy in halo:
        copy.wait()
    outer_patch = (patch == 0) | (patch == 3)
    for f in range(FIELDS):
        mixed = []
        for t in range(2):
            from_l, from_r = from_left[f // 2, t], from_right[f // 2, t]
            if f % 2 == 0:
                two = jnp.where(low_patch, from_l, from_r)
            else:
                two = jnp.where(low_patch, from_r, from_l)
                two = jnp.where(low_patch, row_roll(two, -2), row_roll(two, 2))
            one = jnp.where(patch == 0, row_roll(two, -1), row_roll(two, 1))
            one = jnp.where(outer_patch, one, zero)
            terms = []
            for axis in range(3):
                slot = t if axis == 0 else axis + 1
                terms.append(mix_v[axis, f, t] + coef_v[3, slot] * two + coef_v[2, slot] * one)
            mixed.append(terms)
        for t in range(2):
            across = row_roll(lane_roll(mixed[1 - t][0], 64), 4)
            y, z = mixed[t][1], mixed[t][2]
            y = jnp.where(mid == 0, lane_roll(y, -56), jnp.where(mid == 7, lane_roll(y, 56), zero))
            z = jnp.where(last == 0, lane_roll(z, -7), jnp.where(last == 7, lane_roll(z, 7), zero))
            lift = lift_v[f, t] + across + y + z
            lift_v[f, t] = lift
            state_v[f, t] = state_v[f, t] + step_v[0] * lift

    def advance(m):
        state = get(state_v)
        rate = adjoint_rate(state)
        for f in range(FIELDS):
            for t in range(2):
                x = state[f][t]
                if m < 3:
                    sum_v[f, t] = sum_v[f, t] + step_v[m] * x
                state_v[f, t] = x + step_v[m] * (rate[f][t] + lift_v[f, t])

    advance(1)
    advance(2)

    for t in range(2):
        a = [sum_v[f, t] + step_v[3] * state_v[f, t] for f in range(FIELDS)]
        rows = (
            (a[3] + a[4] + a[5]) * slope_v[0, t],
            sum(a[3 + k] * slope_v[1 + k, t] for k in range(6)),
            sum(a[i] * slope_v[7 + i, t] for i in range(3)),
        )
        for g in range(3):
            if t == 0:
                near_v[0, near, g] = rows[g]
            else:
                far_v[0, far, g] = rows[g]

    def share_far(n):
        copies = [
            pltpu.make_async_remote_copy(
                src_ref=far_v.at[n, far],
                dst_ref=far_v.at[n, far],
                send_sem=far_send.at[n, k],
                recv_sem=far_recv.at[n, k],
                device_id=at_shot(far_peers[k], near),
                device_id_type=MESH,
            )
            for k in sorted(range(1, n_far), key=lambda k: -min(k, n_far - k))
        ]
        for copy in copies:
            copy.start()
        return copies

    def share_near(n):
        copies = [
            pltpu.make_async_remote_copy(
                src_ref=near_v.at[n, near],
                dst_ref=near_v.at[n, near],
                send_sem=near_send.at[n, k],
                recv_sem=near_recv.at[n, k],
                device_id=at_shot(far, near_peers[k]),
                device_id_type=MESH,
            )
            for k in sorted(range(1, GROUP), key=lambda k: -min(k, GROUP - k))
        ]
        for copy in copies:
            copy.start()
        return copies

    def total(ref, n, count, g):
        out = ref[n, 0, g]
        for k in range(1, count):
            out = out + ref[n, k, g]
        return out

    far_one = share_far(0)
    near_one = share_near(0)

    advance(3)
    for f in range(FIELDS):
        for t in range(2):
            for h in range(2):
                begin = (2 * h + t) * LANES
                out_adj[0, f, :, begin : begin + LANES] = state_v[f, t, 4 * h : 4 * h + 4, :]

    for copy in near_one:
        copy.wait_recv()
    for g in range(3):
        far_v[1, far, g] = total(near_v, 0, GROUP, g)
    far_two = share_far(1)
    for copy in far_one:
        copy.wait_recv()
    for g in range(3):
        near_v[1, near, g] = total(far_v, 0, n_far, g)
    near_two = share_near(1)

    for t, copies, ref, count in ((0, far_two, far_v, n_far), (1, near_two, near_v, GROUP)):
        for copy in copies:
            copy.wait_recv()
        for g in range(3):
            value = total(ref, 1, count, g)
            for h in range(2):
                begin = (2 * h + t) * LANES
                out_grad[g, :, begin : begin + LANES] = value[4 * h : 4 * h + 4]
    for copy in far_one + near_one + far_two + near_two:
        copy.wait_send()


def write_back(state, grads, out_state, out_grads, sem):
    copies = [
        pltpu.make_async_copy(source, target, sem.at[i])
        for i, (source, target) in enumerate(((state, out_state), (grads, out_grads)))
    ]
    for copy in copies:
        copy.start()
    for copy in copies:
        copy.wait()


def shards(n_space, n_shot, *operands):
    material = operands[3]
    n_patch, n_coef = material.shape
    n_far = n_shot // GROUP
    field = (FIELDS, 2, ROWS, LANES)
    halo = (5, 2, ROWS, LANES)
    dma = pltpu.SemaphoreType.DMA
    adjoint, checkpoint = (x.transpose(0, 2, 1, 3) for x in operands[:2])
    new_state, grads = pl.pallas_call(
        functools.partial(kernel, n_space, n_shot),
        out_shape=(
            pltpu.VMEM((1, FIELDS, n_patch, n_coef), F32),
            pltpu.VMEM((3, n_patch, n_coef), F32),
        ),
        in_specs=[pl.BlockSpec(memory_space=pl.ANY)] * 11,
        out_specs=[pl.BlockSpec(memory_space=pltpu.VMEM)] * 2,
        scratch_shapes=[
            pltpu.VMEM((FIELDS, n_patch, n_coef), F32),
            pltpu.VMEM((FIELDS, n_patch, n_coef), BF16),
            pltpu.VMEM((FIELDS, n_patch, n_coef), F32),
            pltpu.VMEM((n_patch, n_coef), F32),
            pltpu.VMEM((n_patch, n_coef), F32),
            pltpu.VMEM((n_patch, n_coef), F32),
            pltpu.SMEM((1, n_patch, FIELDS), jnp.int32),
            pltpu.SMEM((3, 8, 8), F32),
            pltpu.SMEM((n_patch,), jnp.int32),
            pltpu.SMEM((n_patch, 6), jnp.int32),
            pltpu.SMEM((n_patch, 6), jnp.int32),
            pltpu.SMEM((n_patch,), jnp.int32),
            pltpu.VMEM(field, F32),
            pltpu.VMEM(field, F32),
            pltpu.VMEM((10, 2, ROWS, LANES), F32),
            pltpu.VMEM(field, F32),
            pltpu.VMEM((3,) + field, F32),
            pltpu.VMEM(field, F32),
            pltpu.VMEM((4, 4, ROWS, LANES), F32),
            pltpu.VMEM((2, ROWS, LANES), F32),
            pltpu.VMEM((4, ROWS, LANES), F32),
            pltpu.VMEM((3, 2, ROWS, LANES), F32),
            pltpu.VMEM((2, 16, ROWS, LANES), F32),
            pltpu.VMEM((2, 2, 2 * LANES, 2 * LANES), BF16),
            pltpu.VMEM(halo, F32),
            pltpu.VMEM(halo, F32),
            pltpu.VMEM(halo, F32),
            pltpu.VMEM(halo, F32),
            pltpu.VMEM((2, GROUP, 3, ROWS, LANES), F32),
            pltpu.VMEM((2, n_far, 3, ROWS, LANES), F32),
            dma((11,)),
            dma((2,)),
            dma((2,)),
            dma((2, GROUP)),
            dma((2, GROUP)),
            dma((2, n_far)),
            dma((2, n_far)),
        ],
        compiler_params=pltpu.CompilerParams(
            collective_id=0, has_side_effects=True, vmem_limit_bytes=16 * 2**20
        ),
    )(*(pltpu.with_memory_space_constraint(x, pltpu.HBM) for x in (adjoint, checkpoint, *operands[2:])))
    new_state, grads = pl.pallas_call(
        write_back,
        out_shape=(
            jax.ShapeDtypeStruct(new_state.shape, F32),
            jax.ShapeDtypeStruct(grads.shape, F32),
        ),
        in_specs=[pl.BlockSpec(memory_space=pl.ANY)] * 2,
        out_specs=[pl.BlockSpec(memory_space=pl.ANY)] * 2,
        scratch_shapes=[dma((2,))],
        compiler_params=pltpu.CompilerParams(vmem_limit_bytes=16 * 2**20),
    )(new_state, grads)
    return new_state.transpose(0, 2, 1, 3), grads.transpose(1, 0, 2)


def solution(mesh):
    return jax.shard_map(
        functools.partial(shards, mesh.shape["space"], mesh.shape["shot"]),
        mesh=mesh,
        in_specs=(
            P("shot", "space", None, None),
            P("shot", "space", None, None),
            P("shot", "space", None),
            P("space", None),
            P("space", None),
            P("space", None),
            P(),
            P("space"),
            P("space", None),
            P("space", None),
            P("space"),
        ),
        out_specs=(P("shot", "space", None, None), P("space", None, None)),
        check_vma=False,
    )
```

```python
import functools

import jax
import jax.numpy as jnp
from jax import lax
from jax.experimental import pallas as pl
from jax.experimental.pallas import tpu as pltpu
from jax.sharding import PartitionSpec as P

ROWS = 8
LANES = 128
FIELDS = 9
GROUP = 8
PAIR = ((0, 5, 4), (5, 1, 3), (4, 3, 2))
MESH = pl.DeviceIdType.MESH
F32 = jnp.float32
BF16 = jnp.bfloat16


def row_roll(x, shift):
    return pltpu.roll(x, shift % ROWS, 0)


def lane_roll(x, shift):
    return pltpu.roll(x, shift % LANES, 1)


def split_dot(pieces, weights):
    x = jnp.concatenate(pieces, axis=0)
    high = x.astype(BF16)
    low = (x - high.astype(F32)).astype(BF16)
    out = jnp.dot(jnp.concatenate([high, low], axis=1), weights, preferred_element_type=F32)
    out = out[:, :LANES] + out[:, LANES:]
    return [out[ROWS * i : ROWS * (i + 1)] for i in range(len(pieces))]


def along_first(pair, table):
    out = [None, None]
    for t in range(2):
        turned = lane_roll(pair[t], 64)
        for r, base in enumerate((pair[t], turned)):
            swapped = row_roll(base, 4)
            for s, value in enumerate((base, swapped)):
                for u in range(2):
                    term = table[((u * 2 + t) * 2 + r) * 2 + s] * value
                    out[u] = term if out[u] is None else out[u] + term
    return out


def derivatives(groups, table, weights_mid, weights_last):
    first = [along_first(pair, table) for pair in groups[0]]
    results = [first]
    for j, weights in ((1, weights_mid), (2, weights_last)):
        flat = split_dot([tile for pair in groups[j] for tile in pair], weights)
        results.append([[flat[2 * i], flat[2 * i + 1]] for i in range(len(groups[j]))])
    return results


def rate_of(state, lam, mu2, buo, table, weights_mid, weights_last):
    tiles = range(2)
    stress = state[3:]
    scaled = [[mu2[t] * stress[k][t] for t in tiles] for k in range(6)]
    for t in tiles:
        bulk = lam[t] * (stress[0][t] + stress[1][t] + stress[2][t])
        for k in range(3):
            scaled[k][t] = scaled[k][t] + bulk
    moved = [[buo[t] * state[i][t] for t in tiles] for i in range(3)]
    groups = [[scaled[PAIR[i][j]] for i in range(3)] + moved for j in range(3)]
    r = derivatives(groups, table, weights_mid, weights_last)
    out = [[r[0][i][t] + r[1][i][t] + r[2][i][t] for t in tiles] for i in range(3)]
    out += [r[0][3], r[1][4], r[2][5]]
    out.append([r[2][4][t] + r[1][5][t] for t in tiles])
    out.append([r[2][3][t] + r[0][5][t] for t in tiles])
    out.append([r[1][3][t] + r[0][4][t] for t in tiles])
    return out


def kernel(
    n_space,
    n_shot,
    adj_hbm,
    ckpt_hbm,
    scale_hbm,
    lam_hbm,
    mu_hbm,
    buo_hbm,
    stiff_hbm,
    level_hbm,
    npatch_hbm,
    nface_hbm,
    count_hbm,
    out_adj,
    out_grad,
    adj_v,
    ckpt_v,
    ckpt_f,
    lam_v,
    mu_v,
    buo_v,
    scale_s,
    stiff_s,
    level_s,
    npatch_s,
    nface_s,
    count_s,
    state_v,
    sum_v,
    slope_v,
    fwd_v,
    mix_v,
    lift_v,
    coef_v,
    own_v,
    step_v,
    mat_v,
    table_v,
    weight_v,
    send_left,
    send_right,
    from_left,
    from_right,
    near_v,
    far_v,
    in_sem,
    halo_send,
    halo_recv,
    near_send,
    near_recv,
    far_send,
    far_recv,
    answer,
):
    n_far = n_shot // GROUP
    space = lax.axis_index("space")
    shot = lax.axis_index("shot")
    far, near = shot // GROUP, lax.rem(shot, GROUP)
    right, left = lax.rem(space + 1, n_space), lax.rem(space + n_space - 1, n_space)
    near_peers = [lax.rem(near + k, GROUP) for k in range(GROUP)]
    far_peers = [lax.rem(far + k, n_far) for k in range(n_far)]

    def at_shot(far_index, near_index):
        return (space, far_index * GROUP + near_index)

    barrier = pltpu.get_barrier_semaphore()


    def greet(semaphore, device):
        pl.semaphore_signal(semaphore, inc=1, device_id=device, device_id_type=MESH)

    inner_left, inner_right = space > 0, space < n_space - 1
    pl.when(inner_left)(functools.partial(greet, barrier, (left, shot)))
    pl.when(inner_right)(functools.partial(greet, barrier, (right, shot)))
    for k in range(1, n_far):
        pl.when(far + k < n_far)(functools.partial(greet, barrier, at_shot(far_peers[k], near)))
    for k in range(1, GROUP):
        greet(barrier, at_shot(far, near_peers[k]))

    loads = [
        pltpu.make_async_copy(source, target, in_sem.at[i])
        for i, (source, target) in enumerate(
            (
                (adj_hbm.at[0], adj_v),
                (ckpt_hbm.at[0], ckpt_v),
                (lam_hbm, lam_v),
                (mu_hbm, mu_v),
                (buo_hbm, buo_v),
                (scale_hbm, scale_s),
                (stiff_hbm, stiff_s),
                (level_hbm, level_s),
                (npatch_hbm, npatch_s),
                (nface_hbm, nface_s),
                (count_hbm, count_s),
            )
        )
    ]
    for load in loads:
        load.start()

    row = lax.broadcasted_iota(jnp.int32, (ROWS, LANES), 0)
    lane = lax.broadcasted_iota(jnp.int32, (ROWS, LANES), 1)
    patch = row & 3
    half = row >> 2
    side = lane >> 6
    mid = (lane >> 3) & 7
    last = lane & 7

    def by_patch(values):
        out = jnp.where(patch == 0, values[0], values[1])
        out = jnp.where(patch == 2, values[2], out)
        return jnp.where(patch == 3, values[3], out)

    def tile(ref, t):
        low = ref[:, t * LANES : (t + 1) * LANES]
        high = ref[:, (2 + t) * LANES : (3 + t) * LANES]
        return jnp.concatenate([low, high], axis=0)

    @pl.when(space == 0)
    def _():
        from_left[...] = jnp.zeros_like(from_left)

    @pl.when(space == n_space - 1)
    def _():
        from_right[...] = jnp.zeros_like(from_right)

    loads[0].wait()
    for f in range(FIELDS):
        for t in range(2):
            state_v[f, t] = tile(adj_v.at[f], t)
    for i in range(5):
        for t in range(2):
            even = state_v[2 * i, t]
            odd = state_v[2 * i + 1, t] if 2 * i + 1 < FIELDS else even
            send_right[i, t] = jnp.where(patch < 2, row_roll(even, -2), odd)
            send_left[i, t] = jnp.where(patch < 2, odd, row_roll(even, 2))

    sides = (space + n_space - 1) // n_space + (2 * n_space - 2 - space) // n_space
    pl.semaphore_wait(barrier, sides + (GROUP - 1) + far)
    halo = [
        pltpu.make_async_remote_copy(
            src_ref=source,
            dst_ref=target,
            send_sem=halo_send.at[i],
            recv_sem=halo_recv.at[i],
            device_id=(device, shot),
            device_id_type=MESH,
        )
        for i, (source, target, device) in enumerate(
            ((send_right, from_left, right), (send_left, from_right, left))
        )
    ]
    pl.when(inner_right)(halo[0].start)
    pl.when(inner_left)(halo[1].start)
    for k in range(1, n_far):
        pl.when(far >= k)(functools.partial(greet, answer, at_shot(far_peers[n_far - k], near)))

    for load in loads[1:]:
        load.wait()

    first_patch = 4 * space
    here = first_patch + patch
    entries = [
        (
            by_patch([nface_s[p, k] for p in range(4)]),
            by_patch([npatch_s[p, k] for p in range(4)]) - here,
        )
        for k in range(6)
    ]
    live_count = by_patch([count_s[p] for p in range(4)])
    offsets = []
    for f in range(6):
        offset = jnp.zeros((ROWS, LANES), jnp.int32)
        for k in range(6):
            face, distance = entries[k]
            offset = jnp.where((face == f) & (k < live_count), distance, offset)
        offsets.append(offset)
    even_patch = (patch & 1) == 0
    low_patch = patch < 2
    candidates = (
        jnp.where(even_patch, 1, -1),
        jnp.where(low_patch, 2, -2),
        jnp.where(even_patch, -1, 1),
        jnp.where(low_patch, -2, 2),
    )
    zero = jnp.zeros((ROWS, LANES), F32)
    first_low = [(half == 0) & (side == 0), None]
    first_high = [None, (half == 1) & (side == 1)]
    for n, wanted in enumerate(candidates):
        weight = [jnp.where(offsets[f] == wanted, 0.5, 0.0) for f in range(6)]
        coef_v[n, 0] = jnp.where(first_low[0], weight[1], zero)
        coef_v[n, 1] = jnp.where(first_high[1], weight[0], zero)
        coef_v[n, 2] = jnp.where(mid == 7, weight[2], jnp.where(mid == 0, weight[3], zero))
        coef_v[n, 3] = jnp.where(last == 7, weight[4], jnp.where(last == 0, weight[5], zero))
    live = [jnp.where(offsets[f] != 0, 0.5, 0.0) for f in range(6)]
    own_rest = (
        jnp.where(mid == 0, live[2], zero)
        + jnp.where(mid == 7, live[3], zero)
        + jnp.where(last == 0, live[4], zero)
        + jnp.where(last == 7, live[5], zero)
    )
    own_v[0] = own_rest + jnp.where(first_low[0], live[0], zero)
    own_v[1] = own_rest + jnp.where(first_high[1], live[1], zero)

    level = by_patch([level_s[p] for p in range(4)])
    step = 0.2 / level.astype(F32)
    for m in range(4):
        step_v[m] = jnp.where(m < level, step, zero)
    for n, (ref, factor) in enumerate(((lam_v, 1.0), (mu_v, 2.0), (buo_v, 1.0))):
        for t in range(2):
            mat_v[n, t] = tile(ref, t) * factor
    for kind in range(2):
        for u in range(2):
            for t in range(2):
                for r in range(2):
                    for s in range(2):
                        picks = []
                        for h in range(2):
                            for e in range(2):
                                source = 4 * (h ^ s) + 2 * t + (e ^ r)
                                target = 4 * h + 2 * u + e
                                if kind == 0:
                                    picks.append(stiff_s[0, target, source])
                                else:
                                    picks.append(stiff_s[0, source, target])
                        low = jnp.where(side == 0, picks[0], picks[1])
                        high = jnp.where(side == 0, picks[2], picks[3])
                        table_v[kind, ((u * 2 + t) * 2 + r) * 2 + s] = jnp.where(half == 0, low, high)

    tall = lax.broadcasted_iota(jnp.int32, (LANES, LANES), 0)
    wide = lax.broadcasted_iota(jnp.int32, (LANES, LANES), 1)
    mid_mask = ((tall >> 6) == (wide >> 6)) & ((tall & 7) == (wide & 7))
    last_mask = (tall >> 3) == (wide >> 3)
    for kind in range(2):
        for n in range(2):
            j = n + 1
            place = mid if n == 0 else last
            spread = zero
            for a in range(8):
                line = zero
                for d in range(8):
                    value = stiff_s[j, d, a] if kind == 0 else stiff_s[j, a, d]
                    line = jnp.where(place == d, value, line)
                spread = jnp.where(row == a, line, spread)
            if n == 0:
                square = jnp.concatenate(
                    [jnp.broadcast_to(spread[a : a + 1], (ROWS, LANES)) for a in range(8)] * 2, axis=0
                )
                square = jnp.where(mid_mask, square, 0.0)
            else:
                square = jnp.where(last_mask, jnp.concatenate([spread] * 16, axis=0), 0.0)
            high = square.astype(BF16)
            low = (square - high.astype(F32)).astype(BF16)
            weight_v[kind, n, :LANES, :LANES] = high
            weight_v[kind, n, LANES:, :LANES] = high
            weight_v[kind, n, :LANES, LANES:] = low
            weight_v[kind, n, LANES:, LANES:] = low

    def get(ref):
        return [[ref[f, t] for t in range(2)] for f in range(FIELDS)]

    def adjoint_rate(state):
        return rate_of(
            state,
            [mat_v[0, t] for t in range(2)],
            [mat_v[1, t] for t in range(2)],
            [mat_v[2, t] for t in range(2)],
            [table_v[0, i] for i in range(16)],
            weight_v[0, 0],
            weight_v[0, 1],
        )

    for f in range(FIELDS):
        for t in range(2):
            x = state_v[f, t]
            back, ahead = row_roll(x, -1), row_roll(x, 1)
            inner = (
                jnp.where(even_patch, back, ahead),
                jnp.where(low_patch, row_roll(x, -2), row_roll(x, 2)),
                jnp.where((patch == 0) | (patch == 3), zero, jnp.where(patch == 1, back, ahead)),
            )
            for axis in range(3):
                slot = t if axis == 0 else axis + 1
                mix_v[axis, f, t] = sum(coef_v[n, slot] * inner[n] for n in range(3))
    start = get(state_v)
    rate = adjoint_rate(start)
    for f in range(FIELDS):
        for t in range(2):
            x = start[f][t]
            sum_v[f, t] = step_v[0] * x
            lift_v[f, t] = -own_v[t] * x
            state_v[f, t] = x + step_v[0] * rate[f][t]

    ckpt_f[...] = ckpt_v[...].astype(F32)
    for f in range(FIELDS):
        power = by_patch([scale_s[0, p, f] for p in range(4)])
        power = lax.shift_left(jnp.ones((ROWS, LANES), jnp.int32), power + 2).astype(F32) * 0.25
        for t in range(2):
            fwd_v[f, t] = tile(ckpt_f.at[f], t) * power
    fields = get(fwd_v)
    groups = [fields[:3] + [fields[3 + PAIR[i][j]] for i in range(3)] for j in range(3)]
    d = derivatives(groups, [table_v[1, i] for i in range(16)], weight_v[1, 0], weight_v[1, 1])
    for t in range(2):
        slope_v[0, t] = d[0][0][t] + d[1][1][t] + d[2][2][t]
        slope_v[1, t] = 2.0 * d[0][0][t]
        slope_v[2, t] = 2.0 * d[1][1][t]
        slope_v[3, t] = 2.0 * d[2][2][t]
        slope_v[4, t] = d[2][1][t] + d[1][2][t]
        slope_v[5, t] = d[2][0][t] + d[0][2][t]
        slope_v[6, t] = d[1][0][t] + d[0][1][t]
        for i in range(3):
            slope_v[7 + i, t] = d[0][3 + i][t] + d[1][3 + i][t] + d[2][3 + i][t]

    pl.when(inner_left)(halo[0].wait_recv)
    pl.when(inner_right)(halo[1].wait_recv)
    outer_patch = (patch == 0) | (patch == 3)
    for f in range(FIELDS):
        mixed = []
        for t in range(2):
            from_l, from_r = from_left[f // 2, t], from_right[f // 2, t]
            if f % 2 == 0:
                two = jnp.where(low_patch, from_l, from_r)
            else:
                two = jnp.where(low_patch, from_r, from_l)
                two = jnp.where(low_patch, row_roll(two, -2), row_roll(two, 2))
            one = jnp.where(patch == 0, row_roll(two, -1), row_roll(two, 1))
            one = jnp.where(outer_patch, one, zero)
            terms = []
            for axis in range(3):
                slot = t if axis == 0 else axis + 1
                terms.append(mix_v[axis, f, t] + coef_v[3, slot] * two + coef_v[2, slot] * one)
            mixed.append(terms)
        for t in range(2):
            across = row_roll(lane_roll(mixed[1 - t][0], 64), 4)
            y, z = mixed[t][1], mixed[t][2]
            y = jnp.where(mid == 0, lane_roll(y, -56), jnp.where(mid == 7, lane_roll(y, 56), zero))
            z = jnp.where(last == 0, lane_roll(z, -7), jnp.where(last == 7, lane_roll(z, 7), zero))
            lift = lift_v[f, t] + across + y + z
            lift_v[f, t] = lift
            state_v[f, t] = state_v[f, t] + step_v[0] * lift

    def advance(m):
        state = get(state_v)
        rate = adjoint_rate(state)
        for f in range(FIELDS):
            for t in range(2):
                x = state[f][t]
                if m < 3:
                    sum_v[f, t] = sum_v[f, t] + step_v[m] * x
                state_v[f, t] = x + step_v[m] * (rate[f][t] + lift_v[f, t])

    advance(1)
    advance(2)

    for t in range(2):
        a = [sum_v[f, t] + step_v[3] * state_v[f, t] for f in range(FIELDS)]
        rows = (
            (a[3] + a[4] + a[5]) * slope_v[0, t],
            sum(a[3 + k] * slope_v[1 + k, t] for k in range(6)),
            sum(a[i] * slope_v[7 + i, t] for i in range(3)),
        )
        for g in range(3):
            if t == 0:
                near_v[0, near, g] = rows[g]
            else:
                far_v[0, far, g] = rows[g]

    def share_far(n):
        order = sorted(range(1, n_far), key=lambda k: -min(k, n_far - k))
        copies = [
            pltpu.make_async_remote_copy(
                src_ref=far_v.at[n, far],
                dst_ref=far_v.at[n, far],
                send_sem=far_send.at[n, k],
                recv_sem=far_recv.at[n, k],
                device_id=at_shot(far_peers[k], near),
                device_id_type=MESH,
            )
            for k in order
        ]
        if n:
            for copy in copies:
                copy.start()
            return copies
        for k, copy in zip(order, copies):
            pl.when(far + k >= n_far)(copy.start)
        pl.when(far < n_far - 1)(lambda: pl.semaphore_wait(answer, n_far - 1 - far))
        for k, copy in zip(order, copies):
            pl.when(far + k < n_far)(copy.start)
        return copies

    def share_near(n):
        copies = [
            pltpu.make_async_remote_copy(
                src_ref=near_v.at[n, near],
                dst_ref=near_v.at[n, near],
                send_sem=near_send.at[n, k],
                recv_sem=near_recv.at[n, k],
                device_id=at_shot(far, near_peers[k]),
                device_id_type=MESH,
            )
            for k in sorted(range(1, GROUP), key=lambda k: -min(k, GROUP - k))
        ]
        for copy in copies:
            copy.start()
        return copies

    def total(ref, n, count, g):
        out = ref[n, 0, g]
        for k in range(1, count):
            out = out + ref[n, k, g]
        return out

    near_one = share_near(0)
    far_one = share_far(0)

    advance(3)
    for f in range(FIELDS):
        for t in range(2):
            for h in range(2):
                begin = (2 * h + t) * LANES
                out_adj[0, f, :, begin : begin + LANES] = state_v[f, t, 4 * h : 4 * h + 4, :]

    for copy in near_one:
        copy.wait_recv()
    for g in range(3):
        far_v[1, far, g] = total(near_v, 0, GROUP, g)
    far_two = share_far(1)
    for copy in far_one:
        copy.wait_recv()
    for g in range(3):
        near_v[1, near, g] = total(far_v, 0, n_far, g)
    near_two = share_near(1)

    for t, copies, ref, count in ((0, far_two, far_v, n_far), (1, near_two, near_v, GROUP)):
        for copy in copies:
            copy.wait_recv()
        for g in range(3):
            value = total(ref, 1, count, g)
            for h in range(2):
                begin = (2 * h + t) * LANES
                out_grad[g, :, begin : begin + LANES] = value[4 * h : 4 * h + 4]
    pl.when(inner_right)(halo[0].wait_send)
    pl.when(inner_left)(halo[1].wait_send)
    for copy in far_one + near_one + far_two + near_two:
        copy.wait_send()


def write_back(state, grads, out_state, out_grads, sem):
    copies = [
        pltpu.make_async_copy(source, target, sem.at[i])
        for i, (source, target) in enumerate(((state, out_state), (grads, out_grads)))
    ]
    for copy in copies:
        copy.start()
    for copy in copies:
        copy.wait()


def shards(n_space, n_shot, *operands):
    material = operands[3]
    n_patch, n_coef = material.shape
    n_far = n_shot // GROUP
    field = (FIELDS, 2, ROWS, LANES)
    halo = (5, 2, ROWS, LANES)
    dma = pltpu.SemaphoreType.DMA
    adjoint, checkpoint = (x.transpose(0, 2, 1, 3) for x in operands[:2])
    new_state, grads = pl.pallas_call(
        functools.partial(kernel, n_space, n_shot),
        out_shape=(
            pltpu.VMEM((1, FIELDS, n_patch, n_coef), F32),
            pltpu.VMEM((3, n_patch, n_coef), F32),
        ),
        in_specs=[pl.BlockSpec(memory_space=pl.ANY)] * 11,
        out_specs=[pl.BlockSpec(memory_space=pltpu.VMEM)] * 2,
        scratch_shapes=[
            pltpu.VMEM((FIELDS, n_patch, n_coef), F32),
            pltpu.VMEM((FIELDS, n_patch, n_coef), BF16),
            pltpu.VMEM((FIELDS, n_patch, n_coef), F32),
            pltpu.VMEM((n_patch, n_coef), F32),
            pltpu.VMEM((n_patch, n_coef), F32),
            pltpu.VMEM((n_patch, n_coef), F32),
            pltpu.SMEM((1, n_patch, FIELDS), jnp.int32),
            pltpu.SMEM((3, 8, 8), F32),
            pltpu.SMEM((n_patch,), jnp.int32),
            pltpu.SMEM((n_patch, 6), jnp.int32),
            pltpu.SMEM((n_patch, 6), jnp.int32),
            pltpu.SMEM((n_patch,), jnp.int32),
            pltpu.VMEM(field, F32),
            pltpu.VMEM(field, F32),
            pltpu.VMEM((10, 2, ROWS, LANES), F32),
            pltpu.VMEM(field, F32),
            pltpu.VMEM((3,) + field, F32),
            pltpu.VMEM(field, F32),
            pltpu.VMEM((4, 4, ROWS, LANES), F32),
            pltpu.VMEM((2, ROWS, LANES), F32),
            pltpu.VMEM((4, ROWS, LANES), F32),
            pltpu.VMEM((3, 2, ROWS, LANES), F32),
            pltpu.VMEM((2, 16, ROWS, LANES), F32),
            pltpu.VMEM((2, 2, 2 * LANES, 2 * LANES), BF16),
            pltpu.VMEM(halo, F32),
            pltpu.VMEM(halo, F32),
            pltpu.VMEM(halo, F32),
            pltpu.VMEM(halo, F32),
            pltpu.VMEM((2, GROUP, 3, ROWS, LANES), F32),
            pltpu.VMEM((2, n_far, 3, ROWS, LANES), F32),
            dma((11,)),
            dma((2,)),
            dma((2,)),
            dma((2, GROUP)),
            dma((2, GROUP)),
            dma((2, n_far)),
            dma((2, n_far)),
            pltpu.SemaphoreType.REGULAR,
        ],
        compiler_params=pltpu.CompilerParams(
            collective_id=0, has_side_effects=True, vmem_limit_bytes=16 * 2**20
        ),
    )(*(pltpu.with_memory_space_constraint(x, pltpu.HBM) for x in (adjoint, checkpoint, *operands[2:])))
    new_state, grads = pl.pallas_call(
        write_back,
        out_shape=(
            jax.ShapeDtypeStruct(new_state.shape, F32),
            jax.ShapeDtypeStruct(grads.shape, F32),
        ),
        in_specs=[pl.BlockSpec(memory_space=pl.ANY)] * 2,
        out_specs=[pl.BlockSpec(memory_space=pl.ANY)] * 2,
        scratch_shapes=[dma((2,))],
        compiler_params=pltpu.CompilerParams(vmem_limit_bytes=16 * 2**20),
    )(new_state, grads)
    return new_state.transpose(0, 2, 1, 3), grads.transpose(1, 0, 2)


def solution(mesh):
    return jax.shard_map(
        functools.partial(shards, mesh.shape["space"], mesh.shape["shot"]),
        mesh=mesh,
        in_specs=(
            P("shot", "space", None, None),
            P("shot", "space", None, None),
            P("shot", "space", None),
            P("space", None),
            P("space", None),
            P("space", None),
            P(),
            P("space"),
            P("space", None),
            P("space", None),
            P("space"),
        ),
        out_specs=(P("shot", "space", None, None), P("space", None, None)),
        check_vma=False,
    )
```

```python
import functools

import jax
import jax.numpy as jnp
from jax import lax
from jax.experimental import pallas as pl
from jax.experimental.pallas import tpu as pltpu
from jax.sharding import PartitionSpec as P

ROWS = 8
LANES = 128
FIELDS = 9
GROUP = 8
PAIR = ((0, 5, 4), (5, 1, 3), (4, 3, 2))
MESH = pl.DeviceIdType.MESH
F32 = jnp.float32
BF16 = jnp.bfloat16


def row_roll(x, shift):
    return pltpu.roll(x, shift % ROWS, 0)


def lane_roll(x, shift):
    return pltpu.roll(x, shift % LANES, 1)


def split_dot(pieces, weights):
    x = jnp.concatenate(pieces, axis=0)
    high = x.astype(BF16)
    low = (x - high.astype(F32)).astype(BF16)
    out = jnp.dot(jnp.concatenate([high, low], axis=1), weights, preferred_element_type=F32)
    out = out[:, :LANES] + out[:, LANES:]
    return [out[ROWS * i : ROWS * (i + 1)] for i in range(len(pieces))]


def along_first(pair, table):
    out = [None, None]
    for t in range(2):
        turned = lane_roll(pair[t], 64)
        for r, base in enumerate((pair[t], turned)):
            swapped = row_roll(base, 4)
            for s, value in enumerate((base, swapped)):
                for u in range(2):
                    term = table[((u * 2 + t) * 2 + r) * 2 + s] * value
                    out[u] = term if out[u] is None else out[u] + term
    return out


def derivatives(groups, table, weights_mid, weights_last):
    first = [along_first(pair, table) for pair in groups[0]]
    results = [first]
    for j, weights in ((1, weights_mid), (2, weights_last)):
        flat = split_dot([tile for pair in groups[j] for tile in pair], weights)
        results.append([[flat[2 * i], flat[2 * i + 1]] for i in range(len(groups[j]))])
    return results


def rate_of(state, lam, mu2, buo, table, weights_mid, weights_last):
    tiles = range(2)
    stress = state[3:]
    scaled = [[mu2[t] * stress[k][t] for t in tiles] for k in range(6)]
    for t in tiles:
        bulk = lam[t] * (stress[0][t] + stress[1][t] + stress[2][t])
        for k in range(3):
            scaled[k][t] = scaled[k][t] + bulk
    moved = [[buo[t] * state[i][t] for t in tiles] for i in range(3)]
    groups = [[scaled[PAIR[i][j]] for i in range(3)] + moved for j in range(3)]
    r = derivatives(groups, table, weights_mid, weights_last)
    out = [[r[0][i][t] + r[1][i][t] + r[2][i][t] for t in tiles] for i in range(3)]
    out += [r[0][3], r[1][4], r[2][5]]
    out.append([r[2][4][t] + r[1][5][t] for t in tiles])
    out.append([r[2][3][t] + r[0][5][t] for t in tiles])
    out.append([r[1][3][t] + r[0][4][t] for t in tiles])
    return out


def kernel(
    n_space,
    n_shot,
    adj_hbm,
    ckpt_hbm,
    scale_hbm,
    lam_hbm,
    mu_hbm,
    buo_hbm,
    stiff_hbm,
    level_hbm,
    npatch_hbm,
    nface_hbm,
    count_hbm,
    out_adj,
    out_grad,
    adj_v,
    ckpt_v,
    ckpt_f,
    lam_v,
    mu_v,
    buo_v,
    scale_s,
    stiff_s,
    level_s,
    npatch_s,
    nface_s,
    count_s,
    state_v,
    sum_v,
    slope_v,
    fwd_v,
    mix_v,
    lift_v,
    coef_v,
    own_v,
    step_v,
    mat_v,
    table_v,
    weight_v,
    send_left,
    send_right,
    from_left,
    from_right,
    near_v,
    far_v,
    in_sem,
    halo_send,
    halo_recv,
    near_send,
    near_recv,
    far_send,
    far_recv,
    answer,
    near_answer,
):
    n_far = n_shot // GROUP
    space = lax.axis_index("space")
    shot = lax.axis_index("shot")
    far, near = shot // GROUP, lax.rem(shot, GROUP)
    right, left = lax.rem(space + 1, n_space), lax.rem(space + n_space - 1, n_space)
    near_peers = [lax.rem(near + k, GROUP) for k in range(GROUP)]
    far_peers = [lax.rem(far + k, n_far) for k in range(n_far)]

    def at_shot(far_index, near_index):
        return (space, far_index * GROUP + near_index)

    barrier = pltpu.get_barrier_semaphore()


    def greet(semaphore, device):
        pl.semaphore_signal(semaphore, inc=1, device_id=device, device_id_type=MESH)

    inner_left, inner_right = space > 0, space < n_space - 1
    pl.when(inner_left)(functools.partial(greet, barrier, (left, shot)))
    pl.when(inner_right)(functools.partial(greet, barrier, (right, shot)))
    for k in range(1, n_far):
        pl.when(far + k < n_far)(functools.partial(greet, barrier, at_shot(far_peers[k], near)))
    for k in range(1, GROUP):
        pl.when(near + k < GROUP)(functools.partial(greet, barrier, at_shot(far, near_peers[k])))

    loads = [
        pltpu.make_async_copy(source, target, in_sem.at[i])
        for i, (source, target) in enumerate(
            (
                (adj_hbm.at[0], adj_v),
                (ckpt_hbm.at[0], ckpt_v),
                (lam_hbm, lam_v),
                (mu_hbm, mu_v),
                (buo_hbm, buo_v),
                (scale_hbm, scale_s),
                (stiff_hbm, stiff_s),
                (level_hbm, level_s),
                (npatch_hbm, npatch_s),
                (nface_hbm, nface_s),
                (count_hbm, count_s),
            )
        )
    ]
    for load in loads:
        load.start()

    row = lax.broadcasted_iota(jnp.int32, (ROWS, LANES), 0)
    lane = lax.broadcasted_iota(jnp.int32, (ROWS, LANES), 1)
    patch = row & 3
    half = row >> 2
    side = lane >> 6
    mid = (lane >> 3) & 7
    last = lane & 7

    def by_patch(values):
        out = jnp.where(patch == 0, values[0], values[1])
        out = jnp.where(patch == 2, values[2], out)
        return jnp.where(patch == 3, values[3], out)

    def tile(ref, t):
        low = ref[:, t * LANES : (t + 1) * LANES]
        high = ref[:, (2 + t) * LANES : (3 + t) * LANES]
        return jnp.concatenate([low, high], axis=0)

    @pl.when(space == 0)
    def _():
        from_left[...] = jnp.zeros_like(from_left)

    @pl.when(space == n_space - 1)
    def _():
        from_right[...] = jnp.zeros_like(from_right)

    loads[0].wait()
    for f in range(FIELDS):
        for t in range(2):
            state_v[f, t] = tile(adj_v.at[f], t)
    for i in range(5):
        for t in range(2):
            even = state_v[2 * i, t]
            odd = state_v[2 * i + 1, t] if 2 * i + 1 < FIELDS else even
            send_right[i, t] = jnp.where(patch < 2, row_roll(even, -2), odd)
            send_left[i, t] = jnp.where(patch < 2, odd, row_roll(even, 2))

    sides = (space + n_space - 1) // n_space + (2 * n_space - 2 - space) // n_space
    pl.semaphore_wait(barrier, sides + near + far)
    halo = [
        pltpu.make_async_remote_copy(
            src_ref=source,
            dst_ref=target,
            send_sem=halo_send.at[i],
            recv_sem=halo_recv.at[i],
            device_id=(device, shot),
            device_id_type=MESH,
        )
        for i, (source, target, device) in enumerate(
            ((send_right, from_left, right), (send_left, from_right, left))
        )
    ]
    pl.when(inner_right)(halo[0].start)
    pl.when(inner_left)(halo[1].start)
    for k in range(1, n_far):
        pl.when(far >= k)(functools.partial(greet, answer, at_shot(far_peers[n_far - k], near)))
    for k in range(1, GROUP):
        pl.when(near >= k)(functools.partial(greet, near_answer, at_shot(far, near_peers[GROUP - k])))

    for load in loads[1:]:
        load.wait()

    first_patch = 4 * space
    here = first_patch + patch
    entries = [
        (
            by_patch([nface_s[p, k] for p in range(4)]),
            by_patch([npatch_s[p, k] for p in range(4)]) - here,
        )
        for k in range(6)
    ]
    live_count = by_patch([count_s[p] for p in range(4)])
    offsets = []
    for f in range(6):
        offset = jnp.zeros((ROWS, LANES), jnp.int32)
        for k in range(6):
            face, distance = entries[k]
            offset = jnp.where((face == f) & (k < live_count), distance, offset)
        offsets.append(offset)
    even_patch = (patch & 1) == 0
    low_patch = patch < 2
    candidates = (
        jnp.where(even_patch, 1, -1),
        jnp.where(low_patch, 2, -2),
        jnp.where(even_patch, -1, 1),
        jnp.where(low_patch, -2, 2),
    )
    zero = jnp.zeros((ROWS, LANES), F32)
    first_low = [(half == 0) & (side == 0), None]
    first_high = [None, (half == 1) & (side == 1)]
    for n, wanted in enumerate(candidates):
        weight = [jnp.where(offsets[f] == wanted, 0.5, 0.0) for f in range(6)]
        coef_v[n, 0] = jnp.where(first_low[0], weight[1], zero)
        coef_v[n, 1] = jnp.where(first_high[1], weight[0], zero)
        coef_v[n, 2] = jnp.where(mid == 7, weight[2], jnp.where(mid == 0, weight[3], zero))
        coef_v[n, 3] = jnp.where(last == 7, weight[4], jnp.where(last == 0, weight[5], zero))
    live = [jnp.where(offsets[f] != 0, 0.5, 0.0) for f in range(6)]
    own_rest = (
        jnp.where(mid == 0, live[2], zero)
        + jnp.where(mid == 7, live[3], zero)
        + jnp.where(last == 0, live[4], zero)
        + jnp.where(last == 7, live[5], zero)
    )
    own_v[0] = own_rest + jnp.where(first_low[0], live[0], zero)
    own_v[1] = own_rest + jnp.where(first_high[1], live[1], zero)

    level = by_patch([level_s[p] for p in range(4)])
    step = 0.2 / level.astype(F32)
    for m in range(4):
        step_v[m] = jnp.where(m < level, step, zero)
    for n, (ref, factor) in enumerate(((lam_v, 1.0), (mu_v, 2.0), (buo_v, 1.0))):
        for t in range(2):
            mat_v[n, t] = tile(ref, t) * factor
    for kind in range(2):
        for u in range(2):
            for t in range(2):
                for r in range(2):
                    for s in range(2):
                        picks = []
                        for h in range(2):
                            for e in range(2):
                                source = 4 * (h ^ s) + 2 * t + (e ^ r)
                                target = 4 * h + 2 * u + e
                                if kind == 0:
                                    picks.append(stiff_s[0, target, source])
                                else:
                                    picks.append(stiff_s[0, source, target])
                        low = jnp.where(side == 0, picks[0], picks[1])
                        high = jnp.where(side == 0, picks[2], picks[3])
                        table_v[kind, ((u * 2 + t) * 2 + r) * 2 + s] = jnp.where(half == 0, low, high)

    tall = lax.broadcasted_iota(jnp.int32, (LANES, LANES), 0)
    wide = lax.broadcasted_iota(jnp.int32, (LANES, LANES), 1)
    mid_mask = ((tall >> 6) == (wide >> 6)) & ((tall & 7) == (wide & 7))
    last_mask = (tall >> 3) == (wide >> 3)
    for kind in range(2):
        for n in range(2):
            j = n + 1
            place = mid if n == 0 else last
            spread = zero
            for a in range(8):
                line = zero
                for d in range(8):
                    value = stiff_s[j, d, a] if kind == 0 else stiff_s[j, a, d]
                    line = jnp.where(place == d, value, line)
                spread = jnp.where(row == a, line, spread)
            if n == 0:
                square = jnp.concatenate(
                    [jnp.broadcast_to(spread[a : a + 1], (ROWS, LANES)) for a in range(8)] * 2, axis=0
                )
                square = jnp.where(mid_mask, square, 0.0)
            else:
                square = jnp.where(last_mask, jnp.concatenate([spread] * 16, axis=0), 0.0)
            high = square.astype(BF16)
            low = (square - high.astype(F32)).astype(BF16)
            weight_v[kind, n, :LANES, :LANES] = high
            weight_v[kind, n, LANES:, :LANES] = high
            weight_v[kind, n, :LANES, LANES:] = low
            weight_v[kind, n, LANES:, LANES:] = low

    def get(ref):
        return [[ref[f, t] for t in range(2)] for f in range(FIELDS)]

    def adjoint_rate(state):
        return rate_of(
            state,
            [mat_v[0, t] for t in range(2)],
            [mat_v[1, t] for t in range(2)],
            [mat_v[2, t] for t in range(2)],
            [table_v[0, i] for i in range(16)],
            weight_v[0, 0],
            weight_v[0, 1],
        )

    for f in range(FIELDS):
        for t in range(2):
            x = state_v[f, t]
            back, ahead = row_roll(x, -1), row_roll(x, 1)
            inner = (
                jnp.where(even_patch, back, ahead),
                jnp.where(low_patch, row_roll(x, -2), row_roll(x, 2)),
                jnp.where((patch == 0) | (patch == 3), zero, jnp.where(patch == 1, back, ahead)),
            )
            for axis in range(3):
                slot = t if axis == 0 else axis + 1
                mix_v[axis, f, t] = sum(coef_v[n, slot] * inner[n] for n in range(3))
    start = get(state_v)
    rate = adjoint_rate(start)
    for f in range(FIELDS):
        for t in range(2):
            x = start[f][t]
            sum_v[f, t] = step_v[0] * x
            lift_v[f, t] = -own_v[t] * x
            state_v[f, t] = x + step_v[0] * rate[f][t]

    ckpt_f[...] = ckpt_v[...].astype(F32)
    for f in range(FIELDS):
        power = by_patch([scale_s[0, p, f] for p in range(4)])
        power = lax.shift_left(jnp.ones((ROWS, LANES), jnp.int32), power + 2).astype(F32) * 0.25
        for t in range(2):
            fwd_v[f, t] = tile(ckpt_f.at[f], t) * power
    fields = get(fwd_v)
    groups = [fields[:3] + [fields[3 + PAIR[i][j]] for i in range(3)] for j in range(3)]
    d = derivatives(groups, [table_v[1, i] for i in range(16)], weight_v[1, 0], weight_v[1, 1])
    for t in range(2):
        slope_v[0, t] = d[0][0][t] + d[1][1][t] + d[2][2][t]
        slope_v[1, t] = 2.0 * d[0][0][t]
        slope_v[2, t] = 2.0 * d[1][1][t]
        slope_v[3, t] = 2.0 * d[2][2][t]
        slope_v[4, t] = d[2][1][t] + d[1][2][t]
        slope_v[5, t] = d[2][0][t] + d[0][2][t]
        slope_v[6, t] = d[1][0][t] + d[0][1][t]
        for i in range(3):
            slope_v[7 + i, t] = d[0][3 + i][t] + d[1][3 + i][t] + d[2][3 + i][t]

    pl.when(inner_left)(halo[0].wait_recv)
    pl.when(inner_right)(halo[1].wait_recv)
    outer_patch = (patch == 0) | (patch == 3)
    for f in range(FIELDS):
        mixed = []
        for t in range(2):
            from_l, from_r = from_left[f // 2, t], from_right[f // 2, t]
            if f % 2 == 0:
                two = jnp.where(low_patch, from_l, from_r)
            else:
                two = jnp.where(low_patch, from_r, from_l)
                two = jnp.where(low_patch, row_roll(two, -2), row_roll(two, 2))
            one = jnp.where(patch == 0, row_roll(two, -1), row_roll(two, 1))
            one = jnp.where(outer_patch, one, zero)
            terms = []
            for axis in range(3):
                slot = t if axis == 0 else axis + 1
                terms.append(mix_v[axis, f, t] + coef_v[3, slot] * two + coef_v[2, slot] * one)
            mixed.append(terms)
        for t in range(2):
            across = row_roll(lane_roll(mixed[1 - t][0], 64), 4)
            y, z = mixed[t][1], mixed[t][2]
            y = jnp.where(mid == 0, lane_roll(y, -56), jnp.where(mid == 7, lane_roll(y, 56), zero))
            z = jnp.where(last == 0, lane_roll(z, -7), jnp.where(last == 7, lane_roll(z, 7), zero))
            lift = lift_v[f, t] + across + y + z
            lift_v[f, t] = lift
            state_v[f, t] = state_v[f, t] + step_v[0] * lift

    def advance(m):
        state = get(state_v)
        rate = adjoint_rate(state)
        for f in range(FIELDS):
            for t in range(2):
                x = state[f][t]
                if m < 3:
                    sum_v[f, t] = sum_v[f, t] + step_v[m] * x
                state_v[f, t] = x + step_v[m] * (rate[f][t] + lift_v[f, t])

    advance(1)
    advance(2)

    for t in range(2):
        a = [sum_v[f, t] + step_v[3] * state_v[f, t] for f in range(FIELDS)]
        rows = (
            (a[3] + a[4] + a[5]) * slope_v[0, t],
            sum(a[3 + k] * slope_v[1 + k, t] for k in range(6)),
            sum(a[i] * slope_v[7 + i, t] for i in range(3)),
        )
        for g in range(3):
            if t == 0:
                near_v[0, near, g] = rows[g]
            else:
                far_v[0, far, g] = rows[g]

    def share_far(n):
        order = range(1, n_far)
        copies = [
            pltpu.make_async_remote_copy(
                src_ref=far_v.at[n, far],
                dst_ref=far_v.at[n, far],
                send_sem=far_send.at[n, k],
                recv_sem=far_recv.at[n, k],
                device_id=at_shot(far_peers[k], near),
                device_id_type=MESH,
            )
            for k in order
        ]
        if n:
            for copy in copies:
                copy.start()
        return copies

    def share_near(n):
        copies = [
            pltpu.make_async_remote_copy(
                src_ref=near_v.at[n, near],
                dst_ref=near_v.at[n, near],
                send_sem=near_send.at[n, k],
                recv_sem=near_recv.at[n, k],
                device_id=at_shot(far, near_peers[k]),
                device_id_type=MESH,
            )
            for k in sorted(range(1, GROUP), key=lambda k: -min(k, GROUP - k))
        ]
        if n:
            for copy in copies:
                copy.start()
        return copies

    def total(ref, n, count, g):
        out = ref[n, 0, g]
        for k in range(1, count):
            out = out + ref[n, k, g]
        return out

    far_one = share_far(0)
    near_one = share_near(0)
    pl.when(near < GROUP - 1)(lambda: pl.semaphore_wait(near_answer, GROUP - 1 - near))
    near_one[0].start()
    for k, copy in enumerate(far_one, 1):
        pl.when(far + k == n_far)(copy.start)
    for copy in near_one[1:3]:
        copy.start()
    for k, copy in enumerate(far_one, 1):
        pl.when(far + k > n_far)(copy.start)
    for copy in near_one[3:]:
        copy.start()
    pl.when(far < n_far - 1)(lambda: pl.semaphore_wait(answer, n_far - 1 - far))
    for k, copy in enumerate(far_one, 1):
        pl.when(far + k < n_far)(copy.start)

    advance(3)
    for f in range(FIELDS):
        for t in range(2):
            for h in range(2):
                begin = (2 * h + t) * LANES
                out_adj[0, f, :, begin : begin + LANES] = state_v[f, t, 4 * h : 4 * h + 4, :]

    for copy in near_one:
        copy.wait_recv()
    for g in range(3):
        far_v[1, far, g] = total(near_v, 0, GROUP, g)
    far_two = share_far(1)
    for copy in far_one:
        copy.wait_recv()
    for g in range(3):
        near_v[1, near, g] = total(far_v, 0, n_far, g)
    near_two = share_near(1)

    pl.when(inner_right)(halo[0].wait_send)
    pl.when(inner_left)(halo[1].wait_send)
    for copy in far_one + near_one + far_two + near_two:
        copy.wait_send()

    for t, copies, ref, count in ((0, far_two, far_v, n_far), (1, near_two, near_v, GROUP)):
        for copy in copies:
            copy.wait_recv()
        for g in range(3):
            value = total(ref, 1, count, g)
            for h in range(2):
                begin = (2 * h + t) * LANES
                out_grad[g, :, begin : begin + LANES] = value[4 * h : 4 * h + 4]


def write_back(state, grads, out_state, out_grads, sem):
    copies = [
        pltpu.make_async_copy(source, target, sem.at[i])
        for i, (source, target) in enumerate(((state, out_state), (grads, out_grads)))
    ]
    for copy in copies:
        copy.start()
    for copy in copies:
        copy.wait()


def shards(n_space, n_shot, *operands):
    material = operands[3]
    n_patch, n_coef = material.shape
    n_far = n_shot // GROUP
    field = (FIELDS, 2, ROWS, LANES)
    halo = (5, 2, ROWS, LANES)
    dma = pltpu.SemaphoreType.DMA
    adjoint, checkpoint = (x.transpose(0, 2, 1, 3) for x in operands[:2])
    new_state, grads = pl.pallas_call(
        functools.partial(kernel, n_space, n_shot),
        out_shape=(
            pltpu.VMEM((1, FIELDS, n_patch, n_coef), F32),
            pltpu.VMEM((3, n_patch, n_coef), F32),
        ),
        in_specs=[pl.BlockSpec(memory_space=pl.ANY)] * 11,
        out_specs=[pl.BlockSpec(memory_space=pltpu.VMEM)] * 2,
        scratch_shapes=[
            pltpu.VMEM((FIELDS, n_patch, n_coef), F32),
            pltpu.VMEM((FIELDS, n_patch, n_coef), BF16),
            pltpu.VMEM((FIELDS, n_patch, n_coef), F32),
            pltpu.VMEM((n_patch, n_coef), F32),
            pltpu.VMEM((n_patch, n_coef), F32),
            pltpu.VMEM((n_patch, n_coef), F32),
            pltpu.SMEM((1, n_patch, FIELDS), jnp.int32),
            pltpu.SMEM((3, 8, 8), F32),
            pltpu.SMEM((n_patch,), jnp.int32),
            pltpu.SMEM((n_patch, 6), jnp.int32),
            pltpu.SMEM((n_patch, 6), jnp.int32),
            pltpu.SMEM((n_patch,), jnp.int32),
            pltpu.VMEM(field, F32),
            pltpu.VMEM(field, F32),
            pltpu.VMEM((10, 2, ROWS, LANES), F32),
            pltpu.VMEM(field, F32),
            pltpu.VMEM((3,) + field, F32),
            pltpu.VMEM(field, F32),
            pltpu.VMEM((4, 4, ROWS, LANES), F32),
            pltpu.VMEM((2, ROWS, LANES), F32),
            pltpu.VMEM((4, ROWS, LANES), F32),
            pltpu.VMEM((3, 2, ROWS, LANES), F32),
            pltpu.VMEM((2, 16, ROWS, LANES), F32),
            pltpu.VMEM((2, 2, 2 * LANES, 2 * LANES), BF16),
            pltpu.VMEM(halo, F32),
            pltpu.VMEM(halo, F32),
            pltpu.VMEM(halo, F32),
            pltpu.VMEM(halo, F32),
            pltpu.VMEM((2, GROUP, 3, ROWS, LANES), F32),
            pltpu.VMEM((2, n_far, 3, ROWS, LANES), F32),
            dma((11,)),
            dma((2,)),
            dma((2,)),
            dma((2, GROUP)),
            dma((2, GROUP)),
            dma((2, n_far)),
            dma((2, n_far)),
            pltpu.SemaphoreType.REGULAR,
            pltpu.SemaphoreType.REGULAR,
        ],
        compiler_params=pltpu.CompilerParams(
            collective_id=0, has_side_effects=True, vmem_limit_bytes=16 * 2**20
        ),
    )(*(pltpu.with_memory_space_constraint(x, pltpu.HBM) for x in (adjoint, checkpoint, *operands[2:])))
    new_state, grads = pl.pallas_call(
        write_back,
        out_shape=(
            jax.ShapeDtypeStruct(new_state.shape, F32),
            jax.ShapeDtypeStruct(grads.shape, F32),
        ),
        in_specs=[pl.BlockSpec(memory_space=pl.ANY)] * 2,
        out_specs=[pl.BlockSpec(memory_space=pl.ANY)] * 2,
        scratch_shapes=[dma((2,))],
        compiler_params=pltpu.CompilerParams(vmem_limit_bytes=16 * 2**20),
    )(new_state, grads)
    return new_state.transpose(0, 2, 1, 3), grads.transpose(1, 0, 2)


def solution(mesh):
    return jax.shard_map(
        functools.partial(shards, mesh.shape["space"], mesh.shape["shot"]),
        mesh=mesh,
        in_specs=(
            P("shot", "space", None, None),
            P("shot", "space", None, None),
            P("shot", "space", None),
            P("space", None),
            P("space", None),
            P("space", None),
            P(),
            P("space"),
            P("space", None),
            P("space", None),
            P("space"),
        ),
        out_specs=(P("shot", "space", None, None), P("space", None, None)),
        check_vma=False,
    )
```

```python
import functools

import jax
import jax.numpy as jnp
from jax import lax
from jax.experimental import pallas as pl
from jax.experimental.pallas import tpu as pltpu
from jax.sharding import PartitionSpec as P

ROWS = 8
LANES = 128
FIELDS = 9
GROUP = 8
PAIR = ((0, 5, 4), (5, 1, 3), (4, 3, 2))
MESH = pl.DeviceIdType.MESH
F32 = jnp.float32
BF16 = jnp.bfloat16


def row_roll(x, shift):
    return pltpu.roll(x, shift % ROWS, 0)


def lane_roll(x, shift):
    return pltpu.roll(x, shift % LANES, 1)


def split_dot(pieces, weights):
    x = jnp.concatenate(pieces, axis=0)
    high = x.astype(BF16)
    low = (x - high.astype(F32)).astype(BF16)
    out = jnp.dot(jnp.concatenate([high, low], axis=1), weights, preferred_element_type=F32)
    out = out[:, :LANES] + out[:, LANES:]
    return [out[ROWS * i : ROWS * (i + 1)] for i in range(len(pieces))]


def along_first(pair, table):
    out = [None, None]
    for t in range(2):
        turned = lane_roll(pair[t], 64)
        for r, base in enumerate((pair[t], turned)):
            swapped = row_roll(base, 4)
            for s, value in enumerate((base, swapped)):
                for u in range(2):
                    term = table[((u * 2 + t) * 2 + r) * 2 + s] * value
                    out[u] = term if out[u] is None else out[u] + term
    return out


def derivatives(groups, table, weights_mid, weights_last):
    first = [along_first(pair, table) for pair in groups[0]]
    results = [first]
    for j, weights in ((1, weights_mid), (2, weights_last)):
        flat = split_dot([tile for pair in groups[j] for tile in pair], weights)
        results.append([[flat[2 * i], flat[2 * i + 1]] for i in range(len(groups[j]))])
    return results


def rate_of(state, lam, mu2, buo, table, weights_mid, weights_last):
    tiles = range(2)
    stress = state[3:]
    scaled = [[mu2[t] * stress[k][t] for t in tiles] for k in range(6)]
    for t in tiles:
        bulk = lam[t] * (stress[0][t] + stress[1][t] + stress[2][t])
        for k in range(3):
            scaled[k][t] = scaled[k][t] + bulk
    moved = [[buo[t] * state[i][t] for t in tiles] for i in range(3)]
    groups = [[scaled[PAIR[i][j]] for i in range(3)] + moved for j in range(3)]
    r = derivatives(groups, table, weights_mid, weights_last)
    out = [[r[0][i][t] + r[1][i][t] + r[2][i][t] for t in tiles] for i in range(3)]
    out += [r[0][3], r[1][4], r[2][5]]
    out.append([r[2][4][t] + r[1][5][t] for t in tiles])
    out.append([r[2][3][t] + r[0][5][t] for t in tiles])
    out.append([r[1][3][t] + r[0][4][t] for t in tiles])
    return out


def kernel(
    n_space,
    n_shot,
    adj_hbm,
    ckpt_hbm,
    scale_hbm,
    lam_hbm,
    mu_hbm,
    buo_hbm,
    stiff_hbm,
    level_hbm,
    npatch_hbm,
    nface_hbm,
    count_hbm,
    out_adj,
    out_grad,
    adj_v,
    ckpt_v,
    ckpt_f,
    lam_v,
    mu_v,
    buo_v,
    scale_s,
    stiff_s,
    level_s,
    npatch_s,
    nface_s,
    count_s,
    state_v,
    sum_v,
    slope_v,
    fwd_v,
    mix_v,
    lift_v,
    coef_v,
    own_v,
    step_v,
    mat_v,
    table_v,
    weight_v,
    send_left,
    send_right,
    from_left,
    from_right,
    near_v,
    far_v,
    in_sem,
    halo_send,
    halo_recv,
    near_send,
    near_recv,
    far_send,
    far_recv,
    answer,
    near_answer,
):
    n_far = n_shot // GROUP
    space = lax.axis_index("space")
    shot = lax.axis_index("shot")
    far, near = shot // GROUP, lax.rem(shot, GROUP)
    right, left = space + 1, space - 1
    near_peers = [lax.rem(near + k, GROUP) for k in range(GROUP)]
    far_peers = [lax.rem(far + k, n_far) for k in range(n_far)]

    def at_shot(far_index, near_index):
        return (space, far_index * GROUP + near_index)

    barrier = pltpu.get_barrier_semaphore()


    def greet(semaphore, device):
        pl.semaphore_signal(semaphore, inc=1, device_id=device, device_id_type=MESH)

    inner_left, inner_right = space > 0, space < n_space - 1
    pl.when(inner_left)(functools.partial(greet, barrier, (left, shot)))
    pl.when(inner_right)(functools.partial(greet, barrier, (right, shot)))
    for k in range(1, n_far):
        pl.when(far + k < n_far)(functools.partial(greet, barrier, at_shot(far_peers[k], near)))
    for k in range(1, GROUP):
        pl.when(near + k < GROUP)(functools.partial(greet, barrier, at_shot(far, near_peers[k])))

    loads = [
        pltpu.make_async_copy(source, target, in_sem.at[i])
        for i, (source, target) in enumerate(
            (
                (adj_hbm.at[0], adj_v),
                (ckpt_hbm.at[0], ckpt_v),
                (lam_hbm, lam_v),
                (mu_hbm, mu_v),
                (buo_hbm, buo_v),
                (scale_hbm, scale_s),
                (stiff_hbm, stiff_s),
                (level_hbm, level_s),
                (npatch_hbm, npatch_s),
                (nface_hbm, nface_s),
                (count_hbm, count_s),
            )
        )
    ]
    for load in loads:
        load.start()

    row = lax.broadcasted_iota(jnp.int32, (ROWS, LANES), 0)
    lane = lax.broadcasted_iota(jnp.int32, (ROWS, LANES), 1)
    patch = row & 3
    half = row >> 2
    side = lane >> 6
    mid = (lane >> 3) & 7
    last = lane & 7

    def by_patch(values):
        out = jnp.where(patch == 0, values[0], values[1])
        out = jnp.where(patch == 2, values[2], out)
        return jnp.where(patch == 3, values[3], out)

    def tile(ref, t):
        low = ref[:, t * LANES : (t + 1) * LANES]
        high = ref[:, (2 + t) * LANES : (3 + t) * LANES]
        return jnp.concatenate([low, high], axis=0)

    @pl.when(space == 0)
    def _():
        from_left[...] = jnp.zeros_like(from_left)

    @pl.when(space == n_space - 1)
    def _():
        from_right[...] = jnp.zeros_like(from_right)

    loads[0].wait()
    for f in range(FIELDS):
        for t in range(2):
            state_v[f, t] = tile(adj_v.at[f], t)
    for f in range(FIELDS):
        send_right[f] = jnp.where(patch < 2, row_roll(state_v[f, 0], -2), state_v[f, 1])
        send_left[f] = jnp.where(patch < 2, state_v[f, 1], row_roll(state_v[f, 0], 2))

    sides = (space + n_space - 1) // n_space + (2 * n_space - 2 - space) // n_space
    pl.semaphore_wait(barrier, sides + near + far)
    halo = [
        pltpu.make_async_remote_copy(
            src_ref=source,
            dst_ref=target,
            send_sem=halo_send.at[i],
            recv_sem=halo_recv.at[i],
            device_id=(device, shot),
            device_id_type=MESH,
        )
        for i, (source, target, device) in enumerate(
            ((send_right, from_left, right), (send_left, from_right, left))
        )
    ]
    pl.when(inner_right)(halo[0].start)
    pl.when(inner_left)(halo[1].start)
    for k in range(1, n_far):
        pl.when(far >= k)(functools.partial(greet, answer, at_shot(far_peers[n_far - k], near)))
    for k in range(1, GROUP):
        pl.when(near >= k)(functools.partial(greet, near_answer, at_shot(far, near_peers[GROUP - k])))

    for load in loads[1:]:
        load.wait()

    first_patch = 4 * space
    here = first_patch + patch
    entries = [
        (
            by_patch([nface_s[p, k] for p in range(4)]),
            by_patch([npatch_s[p, k] for p in range(4)]) - here,
        )
        for k in range(6)
    ]
    live_count = by_patch([count_s[p] for p in range(4)])
    offsets = []
    for f in range(6):
        offset = jnp.zeros((ROWS, LANES), jnp.int32)
        for k in range(6):
            face, distance = entries[k]
            offset = jnp.where((face == f) & (k < live_count), distance, offset)
        offsets.append(offset)
    even_patch = (patch & 1) == 0
    low_patch = patch < 2
    candidates = (
        jnp.where(even_patch, 1, -1),
        jnp.where(low_patch, 2, -2),
        jnp.where(even_patch, -1, 1),
        jnp.where(low_patch, -2, 2),
    )
    zero = jnp.zeros((ROWS, LANES), F32)
    first_low = [(half == 0) & (side == 0), None]
    first_high = [None, (half == 1) & (side == 1)]
    for n, wanted in enumerate(candidates):
        weight = [jnp.where(offsets[f] == wanted, 0.5, 0.0) for f in range(6)]
        coef_v[n, 0] = jnp.where(first_low[0], weight[1], zero)
        coef_v[n, 1] = jnp.where(first_high[1], weight[0], zero)
        coef_v[n, 2] = jnp.where(mid == 7, weight[2], jnp.where(mid == 0, weight[3], zero))
        coef_v[n, 3] = jnp.where(last == 7, weight[4], jnp.where(last == 0, weight[5], zero))
    live = [jnp.where(offsets[f] != 0, 0.5, 0.0) for f in range(6)]
    own_rest = (
        jnp.where(mid == 0, live[2], zero)
        + jnp.where(mid == 7, live[3], zero)
        + jnp.where(last == 0, live[4], zero)
        + jnp.where(last == 7, live[5], zero)
    )
    own_v[0] = own_rest + jnp.where(first_low[0], live[0], zero)
    own_v[1] = own_rest + jnp.where(first_high[1], live[1], zero)

    level = by_patch([level_s[p] for p in range(4)])
    step = 0.2 / level.astype(F32)
    for m in range(4):
        step_v[m] = jnp.where(m < level, step, zero)
    for n, (ref, factor) in enumerate(((lam_v, 1.0), (mu_v, 2.0), (buo_v, 1.0))):
        for t in range(2):
            mat_v[n, t] = tile(ref, t) * factor
    for kind in range(2):
        for u in range(2):
            for t in range(2):
                for r in range(2):
                    for s in range(2):
                        picks = []
                        for h in range(2):
                            for e in range(2):
                                source = 4 * (h ^ s) + 2 * t + (e ^ r)
                                target = 4 * h + 2 * u + e
                                if kind == 0:
                                    picks.append(stiff_s[0, target, source])
                                else:
                                    picks.append(stiff_s[0, source, target])
                        low = jnp.where(side == 0, picks[0], picks[1])
                        high = jnp.where(side == 0, picks[2], picks[3])
                        table_v[kind, ((u * 2 + t) * 2 + r) * 2 + s] = jnp.where(half == 0, low, high)

    tall = lax.broadcasted_iota(jnp.int32, (LANES, LANES), 0)
    wide = lax.broadcasted_iota(jnp.int32, (LANES, LANES), 1)
    mid_mask = ((tall >> 6) == (wide >> 6)) & ((tall & 7) == (wide & 7))
    last_mask = (tall >> 3) == (wide >> 3)
    for kind in range(2):
        for n in range(2):
            j = n + 1
            place = mid if n == 0 else last
            spread = zero
            for a in range(8):
                line = zero
                for d in range(8):
                    value = stiff_s[j, d, a] if kind == 0 else stiff_s[j, a, d]
                    line = jnp.where(place == d, value, line)
                spread = jnp.where(row == a, line, spread)
            if n == 0:
                square = jnp.concatenate(
                    [jnp.broadcast_to(spread[a : a + 1], (ROWS, LANES)) for a in range(8)] * 2, axis=0
                )
                square = jnp.where(mid_mask, square, 0.0)
            else:
                square = jnp.where(last_mask, jnp.concatenate([spread] * 16, axis=0), 0.0)
            high = square.astype(BF16)
            low = (square - high.astype(F32)).astype(BF16)
            weight_v[kind, n, :LANES, :LANES] = high
            weight_v[kind, n, LANES:, :LANES] = high
            weight_v[kind, n, :LANES, LANES:] = low
            weight_v[kind, n, LANES:, LANES:] = low

    def get(ref):
        return [[ref[f, t] for t in range(2)] for f in range(FIELDS)]

    def adjoint_rate(state):
        return rate_of(
            state,
            [mat_v[0, t] for t in range(2)],
            [mat_v[1, t] for t in range(2)],
            [mat_v[2, t] for t in range(2)],
            [table_v[0, i] for i in range(16)],
            weight_v[0, 0],
            weight_v[0, 1],
        )

    for f in range(FIELDS):
        for t in range(2):
            x = state_v[f, t]
            back, ahead = row_roll(x, -1), row_roll(x, 1)
            inner = (
                jnp.where(even_patch, back, ahead),
                jnp.where(low_patch, row_roll(x, -2), row_roll(x, 2)),
                jnp.where((patch == 0) | (patch == 3), zero, jnp.where(patch == 1, back, ahead)),
            )
            for axis in range(3):
                slot = t if axis == 0 else axis + 1
                mix_v[axis, f, t] = sum(coef_v[n, slot] * inner[n] for n in range(3))
    start = get(state_v)
    rate = adjoint_rate(start)
    for f in range(FIELDS):
        for t in range(2):
            x = start[f][t]
            sum_v[f, t] = step_v[0] * x
            lift_v[f, t] = -own_v[t] * x
            state_v[f, t] = x + step_v[0] * rate[f][t]

    ckpt_f[...] = ckpt_v[...].astype(F32)
    for f in range(FIELDS):
        power = by_patch([scale_s[0, p, f] for p in range(4)])
        power = lax.shift_left(jnp.ones((ROWS, LANES), jnp.int32), power + 2).astype(F32) * 0.25
        for t in range(2):
            fwd_v[f, t] = tile(ckpt_f.at[f], t) * power
    fields = get(fwd_v)
    groups = [fields[:3] + [fields[3 + PAIR[i][j]] for i in range(3)] for j in range(3)]
    d = derivatives(groups, [table_v[1, i] for i in range(16)], weight_v[1, 0], weight_v[1, 1])
    for t in range(2):
        slope_v[0, t] = d[0][0][t] + d[1][1][t] + d[2][2][t]
        slope_v[1, t] = 2.0 * d[0][0][t]
        slope_v[2, t] = 2.0 * d[1][1][t]
        slope_v[3, t] = 2.0 * d[2][2][t]
        slope_v[4, t] = d[2][1][t] + d[1][2][t]
        slope_v[5, t] = d[2][0][t] + d[0][2][t]
        slope_v[6, t] = d[1][0][t] + d[0][1][t]
        for i in range(3):
            slope_v[7 + i, t] = d[0][3 + i][t] + d[1][3 + i][t] + d[2][3 + i][t]

    pl.when(inner_left)(halo[0].wait_recv)
    pl.when(inner_right)(halo[1].wait_recv)
    outer_patch = (patch == 0) | (patch == 3)
    for f in range(FIELDS):
        mixed = []
        for t in range(2):
            from_l, from_r = from_left[f], from_right[f]
            if t == 0:
                two = jnp.where(low_patch, from_l, from_r)
            else:
                two = jnp.where(low_patch, from_r, from_l)
                two = jnp.where(low_patch, row_roll(two, -2), row_roll(two, 2))
            one = jnp.where(patch == 0, row_roll(two, -1), row_roll(two, 1))
            one = jnp.where(outer_patch, one, zero)
            terms = []
            for axis in range(3):
                slot = t if axis == 0 else axis + 1
                terms.append(mix_v[axis, f, t] + coef_v[3, slot] * two + coef_v[2, slot] * one)
            mixed.append(terms)
        for t in range(2):
            across = row_roll(lane_roll(mixed[1 - t][0], 64), 4)
            y, z = mixed[t][1], mixed[t][2]
            y = jnp.where(mid == 0, lane_roll(y, -56), jnp.where(mid == 7, lane_roll(y, 56), zero))
            z = jnp.where(last == 0, lane_roll(z, -7), jnp.where(last == 7, lane_roll(z, 7), zero))
            lift = lift_v[f, t] + across + y + z
            lift_v[f, t] = lift
            state_v[f, t] = state_v[f, t] + step_v[0] * lift

    def advance(m):
        state = get(state_v)
        rate = adjoint_rate(state)
        for f in range(FIELDS):
            for t in range(2):
                x = state[f][t]
                if m < 3:
                    sum_v[f, t] = sum_v[f, t] + step_v[m] * x
                state_v[f, t] = x + step_v[m] * (rate[f][t] + lift_v[f, t])

    advance(1)
    advance(2)

    for t in range(2):
        a = [sum_v[f, t] + step_v[3] * state_v[f, t] for f in range(FIELDS)]
        rows = (
            (a[3] + a[4] + a[5]) * slope_v[0, t],
            sum(a[3 + k] * slope_v[1 + k, t] for k in range(6)),
            sum(a[i] * slope_v[7 + i, t] for i in range(3)),
        )
        for g in range(3):
            if t == 0:
                near_v[0, near, g] = rows[g]
            else:
                far_v[0, far, g] = rows[g]

    def share_far(n):
        order = range(1, n_far)
        copies = [
            pltpu.make_async_remote_copy(
                src_ref=far_v.at[n, far],
                dst_ref=far_v.at[n, far],
                send_sem=far_send.at[n, k],
                recv_sem=far_recv.at[n, k],
                device_id=at_shot(far_peers[k], near),
                device_id_type=MESH,
            )
            for k in order
        ]
        if n:
            for copy in copies:
                copy.start()
        return copies

    def share_near(n):
        copies = [
            pltpu.make_async_remote_copy(
                src_ref=near_v.at[n, near],
                dst_ref=near_v.at[n, near],
                send_sem=near_send.at[n, k],
                recv_sem=near_recv.at[n, k],
                device_id=at_shot(far, near_peers[k]),
                device_id_type=MESH,
            )
            for k in sorted(range(1, GROUP), key=lambda k: -min(k, GROUP - k))
        ]
        if n:
            for copy in copies:
                copy.start()
        return copies

    def total(ref, n, count, g):
        out = ref[n, 0, g]
        for k in range(1, count):
            out = out + ref[n, k, g]
        return out

    far_one = share_far(0)
    near_one = share_near(0)
    pl.when(near < GROUP - 1)(lambda: pl.semaphore_wait(near_answer, GROUP - 1 - near))
    near_one[0].start()
    for k, copy in enumerate(far_one, 1):
        pl.when(far + k == n_far)(copy.start)
    for copy in near_one[1:3]:
        copy.start()
    for k, copy in enumerate(far_one, 1):
        pl.when(far + k > n_far)(copy.start)
    for copy in near_one[3:]:
        copy.start()
    pl.when(far < n_far - 1)(lambda: pl.semaphore_wait(answer, n_far - 1 - far))
    for k, copy in enumerate(far_one, 1):
        pl.when(far + k < n_far)(copy.start)

    advance(3)
    for f in range(FIELDS):
        for t in range(2):
            for h in range(2):
                begin = (2 * h + t) * LANES
                out_adj[0, f, :, begin : begin + LANES] = state_v[f, t, 4 * h : 4 * h + 4, :]

    for copy in near_one:
        copy.wait_recv()
    for g in range(3):
        far_v[1, far, g] = total(near_v, 0, GROUP, g)
    far_two = share_far(1)
    for copy in far_one:
        copy.wait_recv()
    for g in range(3):
        near_v[1, near, g] = total(far_v, 0, n_far, g)
    near_two = share_near(1)

    pl.when(inner_right)(halo[0].wait_send)
    pl.when(inner_left)(halo[1].wait_send)
    for copy in far_one + near_one + far_two + near_two:
        copy.wait_send()

    for t, copies, ref, count in ((0, far_two, far_v, n_far), (1, near_two, near_v, GROUP)):
        for copy in copies:
            copy.wait_recv()
        for g in range(3):
            value = total(ref, 1, count, g)
            for h in range(2):
                begin = (2 * h + t) * LANES
                out_grad[g, :, begin : begin + LANES] = value[4 * h : 4 * h + 4]


def write_back(state, grads, out_state, out_grads, sem):
    copies = [
        pltpu.make_async_copy(source, target, sem.at[i])
        for i, (source, target) in enumerate(((grads, out_grads), (state, out_state)))
    ]
    for copy in copies:
        copy.start()
    for copy in copies:
        copy.wait()


def shards(n_space, n_shot, *operands):
    material = operands[3]
    n_patch, n_coef = material.shape
    n_far = n_shot // GROUP
    field = (FIELDS, 2, ROWS, LANES)
    halo = (FIELDS, ROWS, LANES)
    dma = pltpu.SemaphoreType.DMA
    adjoint, checkpoint = (x.transpose(0, 2, 1, 3) for x in operands[:2])
    new_state, grads = pl.pallas_call(
        functools.partial(kernel, n_space, n_shot),
        out_shape=(
            pltpu.VMEM((1, FIELDS, n_patch, n_coef), F32),
            pltpu.VMEM((3, n_patch, n_coef), F32),
        ),
        in_specs=[pl.BlockSpec(memory_space=pl.ANY)] * 11,
        out_specs=[pl.BlockSpec(memory_space=pltpu.VMEM)] * 2,
        scratch_shapes=[
            pltpu.VMEM((FIELDS, n_patch, n_coef), F32),
            pltpu.VMEM((FIELDS, n_patch, n_coef), BF16),
            pltpu.VMEM((FIELDS, n_patch, n_coef), F32),
            pltpu.VMEM((n_patch, n_coef), F32),
            pltpu.VMEM((n_patch, n_coef), F32),
            pltpu.VMEM((n_patch, n_coef), F32),
            pltpu.SMEM((1, n_patch, FIELDS), jnp.int32),
            pltpu.SMEM((3, 8, 8), F32),
            pltpu.SMEM((n_patch,), jnp.int32),
            pltpu.SMEM((n_patch, 6), jnp.int32),
            pltpu.SMEM((n_patch, 6), jnp.int32),
            pltpu.SMEM((n_patch,), jnp.int32),
            pltpu.VMEM(field, F32),
            pltpu.VMEM(field, F32),
            pltpu.VMEM((10, 2, ROWS, LANES), F32),
            pltpu.VMEM(field, F32),
            pltpu.VMEM((3,) + field, F32),
            pltpu.VMEM(field, F32),
            pltpu.VMEM((4, 4, ROWS, LANES), F32),
            pltpu.VMEM((2, ROWS, LANES), F32),
            pltpu.VMEM((4, ROWS, LANES), F32),
            pltpu.VMEM((3, 2, ROWS, LANES), F32),
            pltpu.VMEM((2, 16, ROWS, LANES), F32),
            pltpu.VMEM((2, 2, 2 * LANES, 2 * LANES), BF16),
            pltpu.VMEM(halo, F32),
            pltpu.VMEM(halo, F32),
            pltpu.VMEM(halo, F32),
            pltpu.VMEM(halo, F32),
            pltpu.VMEM((2, GROUP, 3, ROWS, LANES), F32),
            pltpu.VMEM((2, n_far, 3, ROWS, LANES), F32),
            dma((11,)),
            dma((2,)),
            dma((2,)),
            dma((2, GROUP)),
            dma((2, GROUP)),
            dma((2, n_far)),
            dma((2, n_far)),
            pltpu.SemaphoreType.REGULAR,
            pltpu.SemaphoreType.REGULAR,
        ],
        compiler_params=pltpu.CompilerParams(
            collective_id=0, has_side_effects=True, vmem_limit_bytes=16 * 2**20
        ),
    )(*(pltpu.with_memory_space_constraint(x, pltpu.HBM) for x in (adjoint, checkpoint, *operands[2:])))
    new_state, grads = pl.pallas_call(
        write_back,
        out_shape=(
            jax.ShapeDtypeStruct(new_state.shape, F32),
            jax.ShapeDtypeStruct(grads.shape, F32),
        ),
        in_specs=[pl.BlockSpec(memory_space=pl.ANY)] * 2,
        out_specs=[pl.BlockSpec(memory_space=pl.ANY)] * 2,
        scratch_shapes=[dma((2,))],
        compiler_params=pltpu.CompilerParams(vmem_limit_bytes=16 * 2**20),
    )(new_state, grads)
    return new_state.transpose(0, 2, 1, 3), grads.transpose(1, 0, 2)


def solution(mesh):
    return jax.shard_map(
        functools.partial(shards, mesh.shape["space"], mesh.shape["shot"]),
        mesh=mesh,
        in_specs=(
            P("shot", "space", None, None),
            P("shot", "space", None, None),
            P("shot", "space", None),
            P("space", None),
            P("space", None),
            P("space", None),
            P(),
            P("space"),
            P("space", None),
            P("space", None),
            P("space"),
        ),
        out_specs=(P("shot", "space", None, None), P("space", None, None)),
        check_vma=False,
    )
```

```python
import functools

import jax
import jax.numpy as jnp
from jax import lax
from jax.experimental import pallas as pl
from jax.experimental.pallas import tpu as pltpu
from jax.sharding import PartitionSpec as P

ROWS = 8
LANES = 128
FIELDS = 9
GROUP = 8
PAIR = ((0, 5, 4), (5, 1, 3), (4, 3, 2))
MESH = pl.DeviceIdType.MESH
F32 = jnp.float32
BF16 = jnp.bfloat16


def row_roll(x, shift):
    return pltpu.roll(x, shift % ROWS, 0)


def lane_roll(x, shift):
    return pltpu.roll(x, shift % LANES, 1)


def split_dot(pieces, weights):
    x = jnp.concatenate(pieces, axis=0)
    high = x.astype(BF16)
    low = (x - high.astype(F32)).astype(BF16)
    out = jnp.dot(jnp.concatenate([high, low], axis=1), weights, preferred_element_type=F32)
    out = out[:, :LANES] + out[:, LANES:]
    return [out[ROWS * i : ROWS * (i + 1)] for i in range(len(pieces))]


def along_first(pair, table):
    out = [None, None]
    for t in range(2):
        turned = lane_roll(pair[t], 64)
        for r, base in enumerate((pair[t], turned)):
            swapped = row_roll(base, 4)
            for s, value in enumerate((base, swapped)):
                for u in range(2):
                    term = table[((u * 2 + t) * 2 + r) * 2 + s] * value
                    out[u] = term if out[u] is None else out[u] + term
    return out


def derivatives(groups, table, weights_mid, weights_last):
    first = [along_first(pair, table) for pair in groups[0]]
    results = [first]
    for j, weights in ((1, weights_mid), (2, weights_last)):
        flat = split_dot([tile for pair in groups[j] for tile in pair], weights)
        results.append([[flat[2 * i], flat[2 * i + 1]] for i in range(len(groups[j]))])
    return results


def rate_of(state, lam, mu2, buo, table, weights_mid, weights_last):
    tiles = range(2)
    stress = state[3:]
    scaled = [[mu2[t] * stress[k][t] for t in tiles] for k in range(6)]
    for t in tiles:
        bulk = lam[t] * (stress[0][t] + stress[1][t] + stress[2][t])
        for k in range(3):
            scaled[k][t] = scaled[k][t] + bulk
    moved = [[buo[t] * state[i][t] for t in tiles] for i in range(3)]
    groups = [[scaled[PAIR[i][j]] for i in range(3)] + moved for j in range(3)]
    r = derivatives(groups, table, weights_mid, weights_last)
    out = [[r[0][i][t] + r[1][i][t] + r[2][i][t] for t in tiles] for i in range(3)]
    out += [r[0][3], r[1][4], r[2][5]]
    out.append([r[2][4][t] + r[1][5][t] for t in tiles])
    out.append([r[2][3][t] + r[0][5][t] for t in tiles])
    out.append([r[1][3][t] + r[0][4][t] for t in tiles])
    return out


def kernel(
    n_space,
    n_shot,
    adj_hbm,
    ckpt_hbm,
    scale_hbm,
    lam_hbm,
    mu_hbm,
    buo_hbm,
    stiff_hbm,
    level_hbm,
    npatch_hbm,
    nface_hbm,
    count_hbm,
    out_adj,
    out_grad,
    adj_v,
    ckpt_v,
    ckpt_f,
    lam_v,
    mu_v,
    buo_v,
    scale_s,
    stiff_s,
    level_s,
    npatch_s,
    nface_s,
    count_s,
    state_v,
    sum_v,
    slope_v,
    fwd_v,
    mix_v,
    lift_v,
    coef_v,
    own_v,
    step_v,
    mat_v,
    table_v,
    weight_v,
    send_left,
    send_right,
    from_left,
    from_right,
    near_v,
    far_v,
    in_sem,
    halo_send,
    halo_recv,
    near_send,
    near_recv,
    far_send,
    far_recv,
    answer,
    near_answer,
):
    n_far = n_shot // GROUP
    space = lax.axis_index("space")
    shot = lax.axis_index("shot")
    far, near = shot // GROUP, lax.rem(shot, GROUP)
    right, left = space + 1, space - 1
    near_peers = [lax.rem(near + k, GROUP) for k in range(GROUP)]
    far_peers = [lax.rem(far + k, n_far) for k in range(n_far)]

    def at_shot(far_index, near_index):
        return (space, far_index * GROUP + near_index)

    barrier = pltpu.get_barrier_semaphore()


    def greet(semaphore, device):
        pl.semaphore_signal(semaphore, inc=1, device_id=device, device_id_type=MESH)

    inner_left, inner_right = space > 0, space < n_space - 1
    pl.when(inner_left)(functools.partial(greet, barrier, (left, shot)))
    pl.when(inner_right)(functools.partial(greet, barrier, (right, shot)))
    for k in range(1, n_far):
        pl.when(far + k < n_far)(functools.partial(greet, barrier, at_shot(far_peers[k], near)))
    for k in range(1, GROUP):
        pl.when(near + k < GROUP)(functools.partial(greet, barrier, at_shot(far, near_peers[k])))

    loads = [
        pltpu.make_async_copy(source, target, in_sem.at[i])
        for i, (source, target) in enumerate(
            (
                (adj_hbm.at[0], adj_v),
                (ckpt_hbm.at[0], ckpt_v),
                (lam_hbm, lam_v),
                (mu_hbm, mu_v),
                (buo_hbm, buo_v),
                (scale_hbm, scale_s),
                (stiff_hbm, stiff_s),
                (level_hbm, level_s),
                (npatch_hbm, npatch_s),
                (nface_hbm, nface_s),
                (count_hbm, count_s),
            )
        )
    ]
    for load in loads:
        load.start()

    row = lax.broadcasted_iota(jnp.int32, (ROWS, LANES), 0)
    lane = lax.broadcasted_iota(jnp.int32, (ROWS, LANES), 1)
    patch = row & 3
    half = row >> 2
    side = lane >> 6
    mid = (lane >> 3) & 7
    last = lane & 7

    def by_patch(values):
        out = jnp.where(patch == 0, values[0], values[1])
        out = jnp.where(patch == 2, values[2], out)
        return jnp.where(patch == 3, values[3], out)

    def tile(ref, t):
        low = ref[:, t * LANES : (t + 1) * LANES]
        high = ref[:, (2 + t) * LANES : (3 + t) * LANES]
        return jnp.concatenate([low, high], axis=0)

    @pl.when(space == 0)
    def _():
        from_left[...] = jnp.zeros_like(from_left)

    @pl.when(space == n_space - 1)
    def _():
        from_right[...] = jnp.zeros_like(from_right)

    loads[0].wait()
    for f in range(FIELDS):
        for t in range(2):
            state_v[f, t] = tile(adj_v.at[f], t)
    for f in range(FIELDS):
        send_right[f] = jnp.where(patch < 2, row_roll(state_v[f, 0], -2), state_v[f, 1])
        send_left[f] = jnp.where(patch < 2, state_v[f, 1], row_roll(state_v[f, 0], 2))

    sides = (space + n_space - 1) // n_space + (2 * n_space - 2 - space) // n_space
    pl.semaphore_wait(barrier, sides + near + far)
    halo = [
        pltpu.make_async_remote_copy(
            src_ref=source,
            dst_ref=target,
            send_sem=halo_send.at[i],
            recv_sem=halo_recv.at[i],
            device_id=(device, shot),
            device_id_type=MESH,
        )
        for i, (source, target, device) in enumerate(
            ((send_right, from_left, right), (send_left, from_right, left))
        )
    ]
    pl.when(inner_right)(halo[0].start)
    pl.when(inner_left)(halo[1].start)
    for k in range(1, n_far):
        pl.when(far >= k)(functools.partial(greet, answer, at_shot(far_peers[n_far - k], near)))
    for k in range(1, GROUP):
        pl.when(near >= k)(functools.partial(greet, near_answer, at_shot(far, near_peers[GROUP - k])))

    for load in loads[1:]:
        load.wait()

    first_patch = 4 * space
    here = first_patch + patch
    entries = [
        (
            by_patch([nface_s[p, k] for p in range(4)]),
            by_patch([npatch_s[p, k] for p in range(4)]) - here,
        )
        for k in range(6)
    ]
    live_count = by_patch([count_s[p] for p in range(4)])
    offsets = []
    for f in range(6):
        offset = jnp.zeros((ROWS, LANES), jnp.int32)
        for k in range(6):
            face, distance = entries[k]
            offset = jnp.where((face == f) & (k < live_count), distance, offset)
        offsets.append(offset)
    even_patch = (patch & 1) == 0
    low_patch = patch < 2
    candidates = (
        jnp.where(even_patch, 1, -1),
        jnp.where(low_patch, 2, -2),
        jnp.where(even_patch, -1, 1),
        jnp.where(low_patch, -2, 2),
    )
    zero = jnp.zeros((ROWS, LANES), F32)
    first_low = [(half == 0) & (side == 0), None]
    first_high = [None, (half == 1) & (side == 1)]
    for n, wanted in enumerate(candidates):
        weight = [jnp.where(offsets[f] == wanted, 0.5, 0.0) for f in range(6)]
        coef_v[n, 0] = jnp.where(first_low[0], weight[1], zero)
        coef_v[n, 1] = jnp.where(first_high[1], weight[0], zero)
        coef_v[n, 2] = jnp.where(mid == 7, weight[2], jnp.where(mid == 0, weight[3], zero))
        coef_v[n, 3] = jnp.where(last == 7, weight[4], jnp.where(last == 0, weight[5], zero))
    live = [jnp.where(offsets[f] != 0, 0.5, 0.0) for f in range(6)]
    own_rest = (
        jnp.where(mid == 0, live[2], zero)
        + jnp.where(mid == 7, live[3], zero)
        + jnp.where(last == 0, live[4], zero)
        + jnp.where(last == 7, live[5], zero)
    )
    own_v[0] = own_rest + jnp.where(first_low[0], live[0], zero)
    own_v[1] = own_rest + jnp.where(first_high[1], live[1], zero)

    level = by_patch([level_s[p] for p in range(4)])
    step = 0.2 / level.astype(F32)
    for m in range(4):
        step_v[m] = jnp.where(m < level, step, zero)
    for n, (ref, factor) in enumerate(((lam_v, 1.0), (mu_v, 2.0), (buo_v, 1.0))):
        for t in range(2):
            mat_v[n, t] = tile(ref, t) * factor
    for kind in range(2):
        for u in range(2):
            for t in range(2):
                for r in range(2):
                    for s in range(2):
                        picks = []
                        for h in range(2):
                            for e in range(2):
                                source = 4 * (h ^ s) + 2 * t + (e ^ r)
                                target = 4 * h + 2 * u + e
                                if kind == 0:
                                    picks.append(stiff_s[0, target, source])
                                else:
                                    picks.append(stiff_s[0, source, target])
                        low = jnp.where(side == 0, picks[0], picks[1])
                        high = jnp.where(side == 0, picks[2], picks[3])
                        table_v[kind, ((u * 2 + t) * 2 + r) * 2 + s] = jnp.where(half == 0, low, high)

    tall = lax.broadcasted_iota(jnp.int32, (LANES, LANES), 0)
    wide = lax.broadcasted_iota(jnp.int32, (LANES, LANES), 1)
    mid_mask = ((tall >> 6) == (wide >> 6)) & ((tall & 7) == (wide & 7))
    last_mask = (tall >> 3) == (wide >> 3)
    for kind in range(2):
        for n in range(2):
            j = n + 1
            place = mid if n == 0 else last
            spread = zero
            for a in range(8):
                line = zero
                for d in range(8):
                    value = stiff_s[j, d, a] if kind == 0 else stiff_s[j, a, d]
                    line = jnp.where(place == d, value, line)
                spread = jnp.where(row == a, line, spread)
            if n == 0:
                square = jnp.concatenate(
                    [jnp.broadcast_to(spread[a : a + 1], (ROWS, LANES)) for a in range(8)] * 2, axis=0
                )
                square = jnp.where(mid_mask, square, 0.0)
            else:
                square = jnp.where(last_mask, jnp.concatenate([spread] * 16, axis=0), 0.0)
            high = square.astype(BF16)
            low = (square - high.astype(F32)).astype(BF16)
            weight_v[kind, n, :LANES, :LANES] = high
            weight_v[kind, n, LANES:, :LANES] = high
            weight_v[kind, n, :LANES, LANES:] = low
            weight_v[kind, n, LANES:, LANES:] = low

    def get(ref):
        return [[ref[f, t] for t in range(2)] for f in range(FIELDS)]

    def adjoint_rate(state):
        return rate_of(
            state,
            [mat_v[0, t] for t in range(2)],
            [mat_v[1, t] for t in range(2)],
            [mat_v[2, t] for t in range(2)],
            [table_v[0, i] for i in range(16)],
            weight_v[0, 0],
            weight_v[0, 1],
        )

    for f in range(FIELDS):
        for t in range(2):
            x = state_v[f, t]
            back, ahead = row_roll(x, -1), row_roll(x, 1)
            inner = (
                jnp.where(even_patch, back, ahead),
                jnp.where(low_patch, row_roll(x, -2), row_roll(x, 2)),
                jnp.where((patch == 0) | (patch == 3), zero, jnp.where(patch == 1, back, ahead)),
            )
            for axis in range(3):
                slot = t if axis == 0 else axis + 1
                mix_v[axis, f, t] = sum(coef_v[n, slot] * inner[n] for n in range(3))
    start = get(state_v)
    rate = adjoint_rate(start)
    for f in range(FIELDS):
        for t in range(2):
            x = start[f][t]
            sum_v[f, t] = step_v[0] * x
            lift_v[f, t] = -own_v[t] * x
            state_v[f, t] = x + step_v[0] * rate[f][t]

    ckpt_f[...] = ckpt_v[...].astype(F32)
    for f in range(FIELDS):
        power = by_patch([scale_s[0, p, f] for p in range(4)])
        power = lax.shift_left(jnp.ones((ROWS, LANES), jnp.int32), power + 2).astype(F32) * 0.25
        for t in range(2):
            fwd_v[f, t] = tile(ckpt_f.at[f], t) * power
    fields = get(fwd_v)
    groups = [fields[:3] + [fields[3 + PAIR[i][j]] for i in range(3)] for j in range(3)]
    d = derivatives(groups, [table_v[1, i] for i in range(16)], weight_v[1, 0], weight_v[1, 1])
    for t in range(2):
        slope_v[0, t] = d[0][0][t] + d[1][1][t] + d[2][2][t]
        slope_v[1, t] = 2.0 * d[0][0][t]
        slope_v[2, t] = 2.0 * d[1][1][t]
        slope_v[3, t] = 2.0 * d[2][2][t]
        slope_v[4, t] = d[2][1][t] + d[1][2][t]
        slope_v[5, t] = d[2][0][t] + d[0][2][t]
        slope_v[6, t] = d[1][0][t] + d[0][1][t]
        for i in range(3):
            slope_v[7 + i, t] = d[0][3 + i][t] + d[1][3 + i][t] + d[2][3 + i][t]

    pl.when(inner_left)(halo[0].wait_recv)
    pl.when(inner_right)(halo[1].wait_recv)
    outer_patch = (patch == 0) | (patch == 3)
    state = [[] for _ in range(FIELDS)]
    total_state = [[] for _ in range(FIELDS)]
    for f in range(FIELDS):
        mixed = []
        for t in range(2):
            from_l, from_r = from_left[f], from_right[f]
            if t == 0:
                two = jnp.where(low_patch, from_l, from_r)
            else:
                two = jnp.where(low_patch, from_r, from_l)
                two = jnp.where(low_patch, row_roll(two, -2), row_roll(two, 2))
            one = jnp.where(patch == 0, row_roll(two, -1), row_roll(two, 1))
            one = jnp.where(outer_patch, one, zero)
            terms = []
            for axis in range(3):
                slot = t if axis == 0 else axis + 1
                terms.append(mix_v[axis, f, t] + coef_v[3, slot] * two + coef_v[2, slot] * one)
            mixed.append(terms)
        for t in range(2):
            across = row_roll(lane_roll(mixed[1 - t][0], 64), 4)
            y, z = mixed[t][1], mixed[t][2]
            y = jnp.where(mid == 0, lane_roll(y, -56), jnp.where(mid == 7, lane_roll(y, 56), zero))
            z = jnp.where(last == 0, lane_roll(z, -7), jnp.where(last == 7, lane_roll(z, 7), zero))
            lift = lift_v[f, t] + across + y + z
            lift_v[f, t] = lift
            state[f].append(state_v[f, t] + step_v[0] * lift)
            total_state[f].append(sum_v[f, t] + step_v[1] * state[f][t])

    def advance(m, state):
        rate = adjoint_rate(state)
        return [
            [state[f][t] + step_v[m] * (rate[f][t] + lift_v[f, t]) for t in range(2)]
            for f in range(FIELDS)
        ]

    for m in (1, 2):
        state = advance(m, state)
        total_state = [
            [total_state[f][t] + step_v[m + 1] * state[f][t] for t in range(2)] for f in range(FIELDS)
        ]

    for t in range(2):
        a = [total_state[f][t] for f in range(FIELDS)]
        rows = (
            (a[3] + a[4] + a[5]) * slope_v[0, t],
            sum(a[3 + k] * slope_v[1 + k, t] for k in range(6)),
            sum(a[i] * slope_v[7 + i, t] for i in range(3)),
        )
        for g in range(3):
            if t == 0:
                near_v[0, near, g] = rows[g]
            else:
                far_v[0, far, g] = rows[g]

    def share_far(n):
        order = range(1, n_far)
        copies = [
            pltpu.make_async_remote_copy(
                src_ref=far_v.at[n, far],
                dst_ref=far_v.at[n, far],
                send_sem=far_send.at[n, k],
                recv_sem=far_recv.at[n, k],
                device_id=at_shot(far_peers[k], near),
                device_id_type=MESH,
            )
            for k in order
        ]
        if n:
            for copy in copies:
                copy.start()
        return copies

    def share_near(n):
        copies = [
            pltpu.make_async_remote_copy(
                src_ref=near_v.at[n, near],
                dst_ref=near_v.at[n, near],
                send_sem=near_send.at[n, k],
                recv_sem=near_recv.at[n, k],
                device_id=at_shot(far, near_peers[k]),
                device_id_type=MESH,
            )
            for k in sorted(range(1, GROUP), key=lambda k: -min(k, GROUP - k))
        ]
        if n:
            for copy in copies:
                copy.start()
        return copies

    def total(ref, n, count, g):
        out = ref[n, 0, g]
        for k in range(1, count):
            out = out + ref[n, k, g]
        return out

    far_one = share_far(0)
    near_one = share_near(0)
    pl.when(near < GROUP - 1)(lambda: pl.semaphore_wait(near_answer, GROUP - 1 - near))
    near_one[0].start()
    for k, copy in enumerate(far_one, 1):
        pl.when(far + k == n_far)(copy.start)
    for copy in near_one[1:3]:
        copy.start()
    for k, copy in enumerate(far_one, 1):
        pl.when(far + k > n_far)(copy.start)
    for copy in near_one[3:]:
        copy.start()
    pl.when(far < n_far - 1)(lambda: pl.semaphore_wait(answer, n_far - 1 - far))
    for k, copy in enumerate(far_one, 1):
        pl.when(far + k < n_far)(copy.start)

    state = advance(3, state)
    for f in range(FIELDS):
        for t in range(2):
            for h in range(2):
                begin = (2 * h + t) * LANES
                out_adj[0, f, :, begin : begin + LANES] = state[f][t][4 * h : 4 * h + 4]

    for copy in near_one:
        copy.wait_recv()
    for g in range(3):
        far_v[1, far, g] = total(near_v, 0, GROUP, g)
    far_two = share_far(1)
    for copy in far_one:
        copy.wait_recv()
    for g in range(3):
        near_v[1, near, g] = total(far_v, 0, n_far, g)
    near_two = share_near(1)

    pl.when(inner_right)(halo[0].wait_send)
    pl.when(inner_left)(halo[1].wait_send)
    for copy in far_one + near_one + far_two + near_two:
        copy.wait_send()

    for t, copies, ref, count in ((0, far_two, far_v, n_far), (1, near_two, near_v, GROUP)):
        for copy in copies:
            copy.wait_recv()
        for g in range(3):
            value = total(ref, 1, count, g)
            for h in range(2):
                begin = (2 * h + t) * LANES
                out_grad[g, :, begin : begin + LANES] = value[4 * h : 4 * h + 4]


def write_back(state, grads, out_state, out_grads, sem):
    copies = [
        pltpu.make_async_copy(source, target, sem.at[i])
        for i, (source, target) in enumerate(((grads, out_grads), (state, out_state)))
    ]
    for copy in copies:
        copy.start()
    for copy in copies:
        copy.wait()


def shards(n_space, n_shot, *operands):
    material = operands[3]
    n_patch, n_coef = material.shape
    n_far = n_shot // GROUP
    field = (FIELDS, 2, ROWS, LANES)
    halo = (FIELDS, ROWS, LANES)
    dma = pltpu.SemaphoreType.DMA
    adjoint, checkpoint = (x.transpose(0, 2, 1, 3) for x in operands[:2])
    new_state, grads = pl.pallas_call(
        functools.partial(kernel, n_space, n_shot),
        out_shape=(
            pltpu.VMEM((1, FIELDS, n_patch, n_coef), F32),
            pltpu.VMEM((3, n_patch, n_coef), F32),
        ),
        in_specs=[pl.BlockSpec(memory_space=pl.ANY)] * 11,
        out_specs=[pl.BlockSpec(memory_space=pltpu.VMEM)] * 2,
        scratch_shapes=[
            pltpu.VMEM((FIELDS, n_patch, n_coef), F32),
            pltpu.VMEM((FIELDS, n_patch, n_coef), BF16),
            pltpu.VMEM((FIELDS, n_patch, n_coef), F32),
            pltpu.VMEM((n_patch, n_coef), F32),
            pltpu.VMEM((n_patch, n_coef), F32),
            pltpu.VMEM((n_patch, n_coef), F32),
            pltpu.SMEM((1, n_patch, FIELDS), jnp.int32),
            pltpu.SMEM((3, 8, 8), F32),
            pltpu.SMEM((n_patch,), jnp.int32),
            pltpu.SMEM((n_patch, 6), jnp.int32),
            pltpu.SMEM((n_patch, 6), jnp.int32),
            pltpu.SMEM((n_patch,), jnp.int32),
            pltpu.VMEM(field, F32),
            pltpu.VMEM(field, F32),
            pltpu.VMEM((10, 2, ROWS, LANES), F32),
            pltpu.VMEM(field, F32),
            pltpu.VMEM((3,) + field, F32),
            pltpu.VMEM(field, F32),
            pltpu.VMEM((4, 4, ROWS, LANES), F32),
            pltpu.VMEM((2, ROWS, LANES), F32),
            pltpu.VMEM((4, ROWS, LANES), F32),
            pltpu.VMEM((3, 2, ROWS, LANES), F32),
            pltpu.VMEM((2, 16, ROWS, LANES), F32),
            pltpu.VMEM((2, 2, 2 * LANES, 2 * LANES), BF16),
            pltpu.VMEM(halo, F32),
            pltpu.VMEM(halo, F32),
            pltpu.VMEM(halo, F32),
            pltpu.VMEM(halo, F32),
            pltpu.VMEM((2, GROUP, 3, ROWS, LANES), F32),
            pltpu.VMEM((2, n_far, 3, ROWS, LANES), F32),
            dma((11,)),
            dma((2,)),
            dma((2,)),
            dma((2, GROUP)),
            dma((2, GROUP)),
            dma((2, n_far)),
            dma((2, n_far)),
            pltpu.SemaphoreType.REGULAR,
            pltpu.SemaphoreType.REGULAR,
        ],
        compiler_params=pltpu.CompilerParams(
            collective_id=0, has_side_effects=True, vmem_limit_bytes=16 * 2**20
        ),
    )(*(pltpu.with_memory_space_constraint(x, pltpu.HBM) for x in (adjoint, checkpoint, *operands[2:])))
    new_state, grads = pl.pallas_call(
        write_back,
        out_shape=(
            jax.ShapeDtypeStruct(new_state.shape, F32),
            jax.ShapeDtypeStruct(grads.shape, F32),
        ),
        in_specs=[pl.BlockSpec(memory_space=pl.ANY)] * 2,
        out_specs=[pl.BlockSpec(memory_space=pl.ANY)] * 2,
        scratch_shapes=[dma((2,))],
        compiler_params=pltpu.CompilerParams(vmem_limit_bytes=16 * 2**20),
    )(new_state, grads)
    return new_state.transpose(0, 2, 1, 3), grads.transpose(1, 0, 2)


def solution(mesh):
    return jax.shard_map(
        functools.partial(shards, mesh.shape["space"], mesh.shape["shot"]),
        mesh=mesh,
        in_specs=(
            P("shot", "space", None, None),
            P("shot", "space", None, None),
            P("shot", "space", None),
            P("space", None),
            P("space", None),
            P("space", None),
            P(),
            P("space"),
            P("space", None),
            P("space", None),
            P("space"),
        ),
        out_specs=(P("shot", "space", None, None), P("space", None, None)),
        check_vma=False,
    )
```
